32 devices in a mesh: groups: 2 (over y), seq: 4 (over z), head: 4 (over x, core).
Axes of the slice: x: 2, y: 2, z: 4, core: 2. Of those that a mesh axis runs over, the one named last changes fastest.
Arguments:
- doc_start: int32 [1024], P(('groups', 'seq')), parts along dimension 0, may hold values from 0 to 511, as said below
- q_gdn: bfloat16 [1024, 2048], P(('groups', 'seq'), 'head'), parts along dimension 0, may hold values from -6 to 6
- k_gdn: bfloat16 [1024, 2048], P(('groups', 'seq'), 'head'), parts along dimension 0, may hold values from -6 to 6
- v_gdn: bfloat16 [1024, 4096], P(('groups', 'seq'), 'head'), parts along dimension 0, may hold values from -6 to 6
- z_gdn: bfloat16 [1024, 4096], P(('groups', 'seq'), 'head'), parts along dimension 0, may hold values from -6 to 6
- beta_logit: float32 [32, 1024], P('head', ('groups', 'seq')), parts along dimension 1, may hold values from -8 to 3
- log_decay: float32 [32, 1024], P('head', ('groups', 'seq')), parts along dimension 1, may hold values from -1 to 0
- norm_weight: float32 [128], replicated, may hold values from 0.1 to 1.9
- q_attn: bfloat16 [1024, 4096], P(('groups', 'seq'), 'head'), parts along dimension 0, may hold values from -6 to 6
- k_attn: bfloat16 [1024, 512], P(('groups', 'seq')), parts along dimension 0, may hold values from -6 to 6
- v_attn: bfloat16 [1024, 512], P(('groups', 'seq')), parts along dimension 0, may hold values from -6 to 6
- gate_attn: bfloat16 [1024, 4096], P(('groups', 'seq'), 'head'), parts along dimension 0, may hold values from -6 to 6
Outputs:
- gdn_out: bfloat16 [1024, 4096], P(('groups', 'seq'), 'head'), parts along dimension 0
- attn_out: bfloat16 [1024, 4096], P(('groups', 'seq'), 'head'), parts along dimension 0
The draws below stay inside these ranges and needn't reach their ends.
There are 2 independent parts, one for each index of `groups`. The reference program is written for one: setup_inputs(seed, part) draws one part's arguments, and reference() takes and returns one part's arrays. A program takes and returns all parts, laid end to end along the dimension named above; an argument that names none is the same for every part. Nothing has to cross between parts.
Inputs may be any that keep to these rules, and one draw needn't show every extreme that they name: Nondecreasing; doc_start[i] <= i, with equality exactly at the first token of each of the 3 documents; the first document starts at 0.
All inputs are finite; a program needn't handle non-finite values.
Results may differ from the reference program's by a relative error of at most 0.0095.
Values may be sent and summed in bfloat16 or wider, within the bound.
No kernel may reach another device: no remote copies, remote signals or barrier semaphores. Data moves between devices by JAX's collectives and lax.ppermute only.
A program may use at most 128 MiB of HBM per device.

```python
import jax
import jax.numpy as jnp
from jax import lax

VH = 32
KH = 16
DK = 128
DV = 128
QH = 16
KVH = 2
HD_A = 256
TOK_DEV = 128
NDOCS = 3
TOKENS = 512
WINDOW = 384


def head_speed(key):
    order = jax.random.permutation(jax.random.fold_in(key, 7001), VH)
    count = VH // 2
    return order < count


def draw_log_decay(key, part):
    quick = head_speed(key)
    streams = jax.random.split(jax.random.fold_in(key, 7002), 5)
    blocks = TOKENS // TOK_DEV
    arrival_ratio = jnp.where(quick, 1.0 / 40.0, 0.4 / TOKENS)
    arrival_ratio = arrival_ratio * jax.random.uniform(streams[0], (VH,), minval=0.7, maxval=1.4)
    per_block = jnp.exp(jax.random.uniform(streams[1], (VH, blocks), minval=-0.7, maxval=0.7))
    per_token = jnp.exp(jax.random.uniform(streams[2], (VH, TOKENS), minval=-0.7, maxval=0.7))
    coarse_estimate = jnp.repeat(per_block, TOK_DEV, axis=1) * per_token
    spots = jax.random.randint(streams[3], (2,), 0, TOKENS)
    miss_count = jax.random.uniform(streams[4], (2,), minval=0.2, maxval=0.5)
    place = jnp.arange(TOKENS, dtype=jnp.int32)
    match_count = (place[None, :] == spots[:, None]).astype(jnp.float32)
    sudden_spike = jnp.sum(match_count * jnp.log(1.0 - miss_count)[:, None], axis=0)
    sluggish_level = jnp.where(quick, 0.0, 1.0)
    return -arrival_ratio[:, None] * coarse_estimate + sluggish_level[:, None] * sudden_spike[None, :]


def draw_beta_logit(key, part):
    quick = head_speed(key)
    streams = jax.random.split(jax.random.fold_in(key, 7003), 2)
    fast_level = jax.random.uniform(streams[0], (VH,), minval=0.3, maxval=0.6)
    level = jnp.where(quick, fast_level, 0.5 * DK / TOKENS)
    coarse_estimate = jnp.exp(jax.random.uniform(streams[1], (VH, TOKENS), minval=-0.7, maxval=0.7))
    beta = jnp.minimum(level[:, None] * coarse_estimate, 0.95)
    return jnp.log(beta) - jnp.log1p(-beta)


def draw_doc_start(key, part):
    order = jax.random.permutation(jax.random.fold_in(key, 7004), TOKENS - 1) + 1
    cuts = jnp.sort(order[:NDOCS - 1]).astype(jnp.int32)
    starts = jnp.concatenate([jnp.zeros((1,), jnp.int32), cuts])
    place = jnp.arange(TOKENS, dtype=jnp.int32)
    return jnp.max(jnp.where(starts[None, :] <= place[:, None], starts[None, :], 0), axis=1).astype(jnp.int32)


def draw_q_attn(key, part):
    base_key = jax.random.fold_in(key, 7006)
    width = QH * HD_A
    values = jnp.clip(jax.random.normal(base_key, (TOKENS, width)), -6.0, 6.0)
    return values.astype(jnp.bfloat16)


def draw_k_attn(key, part):
    base_key = jax.random.fold_in(key, 7007)
    width = KVH * HD_A
    values = jnp.clip(jax.random.normal(base_key, (TOKENS, width)), -6.0, 6.0)
    return values.astype(jnp.bfloat16)


def levels(rng, dims, cuts, least, high):
    def one(axis_at, shards_of):
        heights = jax.random.uniform(jax.random.fold_in(jax.random.fold_in(rng, 6), axis_at), (shards_of,), jnp.float32, least / len(cuts), high / len(cuts))
        return jnp.repeat(jnp.exp(heights), dims[axis_at] // shards_of).reshape((-1,) + (1,) * (len(dims) - axis_at - 1))

    loudness = one(*cuts[0])
    for cut in cuts[1:]:
        loudness = loudness * one(*cut)
    return loudness


def normal_values(rng, extent, spread, most, cuts=(), held_as=jnp.bfloat16):
    drawn = jax.random.normal(rng, extent, jnp.float32) * spread
    if len(cuts) > 0:
        drawn = levels(rng, extent, cuts, -0.22, 0.18) * drawn
    return jnp.clip(drawn, min=-most, max=most).astype(held_as)


def setup_inputs(seed: int = 0, part: int = 0) -> dict:
    key_list = jax.random.split(jax.random.key(seed), 13)
    part_splits = jax.random.split(jax.random.fold_in(key_list[12], part), 13)
    return {
        "doc_start": draw_doc_start(jax.random.fold_in(jax.random.fold_in(key_list[12], part), 71), part),
        "q_gdn": normal_values(part_splits[1], (TOKENS, KH * DK), 1.0, 6.0, ((0, 4), (1, 4))),
        "k_gdn": normal_values(part_splits[2], (TOKENS, KH * DK), 1.0, 6.0, ((0, 4), (1, 4))),
        "v_gdn": normal_values(part_splits[3], (TOKENS, VH * DV), 1.0, 6.0, ((0, 4), (1, 4))),
        "z_gdn": normal_values(part_splits[4], (TOKENS, VH * DV), 1.0, 6.0, ((0, 4), (1, 4))),
        "beta_logit": draw_beta_logit(jax.random.fold_in(jax.random.fold_in(key_list[12], part), 71), part),
        "log_decay": draw_log_decay(jax.random.fold_in(jax.random.fold_in(key_list[12], part), 71), part),
        "norm_weight": jnp.clip(1.0 + 0.18 * jax.random.normal(key_list[7], (DV,), jnp.float32), 0.1, 1.9),
        "q_attn": draw_q_attn(jax.random.fold_in(jax.random.fold_in(key_list[12], part), 71), part),
        "k_attn": draw_k_attn(jax.random.fold_in(jax.random.fold_in(key_list[12], part), 71), part),
        "v_attn": normal_values(part_splits[10], (TOKENS, KVH * HD_A), 1.0, 6.0, ((0, 4),)),
        "gate_attn": normal_values(part_splits[11], (TOKENS, QH * HD_A), 1.0, 6.0, ((0, 4), (1, 4))),
    }


HIGH = lax.Precision.HIGHEST

def unit_rows(values):
    return values * lax.rsqrt(lax.optimization_barrier(jnp.sum(values * values, axis=-1, keepdims=True)) + 1e-06)

def delta_rule(doc_start, q_gdn, k_gdn, v_gdn, beta_logit, log_decay):
    length = q_gdn.shape[0]
    repeat = VH // KH
    query = jnp.repeat(unit_rows(q_gdn.astype(jnp.float32).reshape(length, KH, DK)), repeat, axis=1)
    keys = jnp.repeat(unit_rows(k_gdn.astype(jnp.float32).reshape(length, KH, DK)), repeat, axis=1)
    values = v_gdn.astype(jnp.float32).reshape(length, VH, DV)
    beta = jax.nn.sigmoid(beta_logit).T
    decay = jnp.exp(log_decay).T
    place = jnp.arange(length, dtype=jnp.int32)
    carry_on = (doc_start != place).astype(jnp.float32)

    def advance(state, inputs):
        query_t, key_t, value_t, beta_t, decay_t, carry_t = inputs
        state = state * (decay_t * carry_t)[:, None, None]
        guess = jnp.einsum('hvk,hk->hv', state, key_t, precision=HIGH)
        update = beta_t[:, None] * (value_t - guess)
        state = state + update[:, :, None] * key_t[:, None, :]
        return (state, jnp.einsum('hvk,hk->hv', state, query_t, precision=HIGH))
    anchor = jnp.zeros((VH, DV, DK), jnp.float32)
    _, mixed = lax.scan(advance, anchor, (query, keys, values, beta, decay, carry_on))
    return mixed

def gated_norm(mixed, z_gdn, norm_weight):
    length = mixed.shape[0]
    gate = z_gdn.astype(jnp.float32).reshape(length, VH, DV)
    factor = lax.rsqrt(lax.optimization_barrier(jnp.mean(mixed * mixed, axis=-1, keepdims=True)) + 1e-06)
    normed = mixed * factor * norm_weight * jax.nn.silu(gate)
    return normed.reshape(length, VH * DV).astype(jnp.bfloat16)

def window_attention(doc_start, q_attn, k_attn, v_attn, gate_attn):
    length = q_attn.shape[0]
    span = min(WINDOW + TOK_DEV, length)
    group = QH // KVH
    factor = HD_A ** (-0.5)

    def one_block(index):
        q_start = (index * TOK_DEV).astype(jnp.int32)
        k_start = jnp.clip(q_start - WINDOW, 0, length - span).astype(jnp.int32)
        query = lax.dynamic_slice_in_dim(q_attn, q_start, TOK_DEV, 0).astype(jnp.float32).reshape(TOK_DEV, QH, HD_A)
        gate = lax.dynamic_slice_in_dim(gate_attn, q_start, TOK_DEV, 0).astype(jnp.float32).reshape(TOK_DEV, QH, HD_A)
        docs = lax.dynamic_slice_in_dim(doc_start, q_start, TOK_DEV, 0)
        keys = lax.dynamic_slice_in_dim(k_attn, k_start, span, 0).astype(jnp.float32).reshape(span, KVH, HD_A)
        values = lax.dynamic_slice_in_dim(v_attn, k_start, span, 0).astype(jnp.float32).reshape(span, KVH, HD_A)
        keys = jnp.repeat(keys, group, axis=1)
        values = jnp.repeat(values, group, axis=1)
        scores = jnp.einsum('qhd,khd->hqk', query, keys, precision=HIGH) * factor
        q_place = q_start + jnp.arange(TOK_DEV, dtype=jnp.int32)
        k_place = k_start + jnp.arange(span, dtype=jnp.int32)
        lower = jnp.maximum(docs, q_place - WINDOW + 1)
        visible = (k_place[None, :] >= lower[:, None]) & (k_place[None, :] <= q_place[:, None])
        masked = jnp.where(visible[None], scores, -jnp.inf)
        peak = lax.optimization_barrier(jnp.max(masked, axis=-1, keepdims=True))
        weights = jnp.exp(masked - peak)
        total = lax.optimization_barrier(jnp.sum(weights, axis=-1))
        rounded = lax.optimization_barrier(weights.astype(jnp.bfloat16)).astype(jnp.float32)
        mixed = jnp.einsum('hqk,khd->qhd', rounded, values, precision=HIGH)
        result = mixed / total.T[:, :, None] * jax.nn.sigmoid(gate)
        return result.reshape(TOK_DEV, QH * HD_A).astype(jnp.bfloat16)
    blocks = lax.map(one_block, jnp.arange(length // TOK_DEV, dtype=jnp.int32))
    return blocks.reshape(length, QH * HD_A)

def reference(doc_start, q_gdn, k_gdn, v_gdn, z_gdn, beta_logit, log_decay, norm_weight, q_attn, k_attn, v_attn, gate_attn):
    mixed = delta_rule(doc_start, q_gdn, k_gdn, v_gdn, beta_logit, log_decay)
    gdn_out = gated_norm(mixed, z_gdn, norm_weight)
    attn_out = window_attention(doc_start, q_attn, k_attn, v_attn, gate_attn)
    return (gdn_out, attn_out)
```

```python
import functools

import jax
import jax.numpy as jnp
from jax import lax
from jax.experimental import pallas as pl
from jax.experimental.pallas import tpu as pltpu
from jax.sharding import PartitionSpec as P

DK = 128
DV = 128
QH = 16
KVH = 2
HD_A = 256
EPS = 1e-06
VMEM_LIMIT = 48 * 1024 * 1024

F32 = jnp.float32
BF16 = jnp.bfloat16


def dot(a, b):
    return jnp.dot(a, b, preferred_element_type=F32)


def dot_t(a, b):
    return lax.dot_general(a, b, (((1,), (1,)), ((), ())), preferred_element_type=F32)


def prefix_sums(rows):
    count, length = rows.shape
    first = rows.astype(BF16)
    rest = rows - first.astype(F32)
    second = rest.astype(BF16)
    third = (rest - second.astype(F32)).astype(BF16)
    t_at = lax.broadcasted_iota(jnp.int32, (length, length), 0)
    i_at = lax.broadcasted_iota(jnp.int32, (length, length), 1)
    ones = (t_at <= i_at).astype(F32).astype(BF16)
    return dot(first, ones) + dot(second, ones) + dot(third, ones)


def columns_of(rows):
    count, length = rows.shape
    padded = jnp.concatenate([rows, jnp.zeros((length - count, length), F32)], axis=0)
    return padded.T


def diagonal_row(square, same_place):
    return jnp.sum(jnp.where(same_place, square, 0.0), axis=0, keepdims=True)


def places(length):
    row = lax.broadcasted_iota(jnp.int32, (length, length), 0)
    col = lax.broadcasted_iota(jnp.int32, (length, length), 1)
    return row, col


def state_kernel(anchor_ref, doc_ref, beta_ref, gate_ref, k_ref, v_ref, x_ref, u_ref, a_ref, send_ref):
    length = k_ref.shape[0]
    heads = beta_ref.shape[0]
    key_heads = k_ref.shape[1] // DK
    repeat = heads // key_heads
    anchor = anchor_ref[0]
    row, col = places(length)
    beta = jax.nn.sigmoid(beta_ref[...])
    running = prefix_sums(gate_ref[...])
    doc = doc_ref[...]
    keys = [k_ref[:, g * DK : (g + 1) * DK] for g in range(key_heads)]
    grams = [dot_t(k, k) for k in keys]
    squares = [diagonal_row(g, row == col) + EPS for g in grams]
    log_inv = [-0.5 * jnp.log(s) for s in squares]
    inv = [lax.rsqrt(s) for s in squares]
    log_rows = jnp.concatenate([log_inv[h // repeat] for h in range(heads)], axis=0)
    cols = columns_of(
        jnp.concatenate([running + log_rows, jnp.broadcast_to(doc.astype(F32), (8, length))], axis=0)
    )
    doc_col = cols[:, heads : heads + 1]
    place = (anchor + col).astype(F32)
    strict = (doc_col <= place) & (col < row)
    tail_same = doc[:, length - 1 : length] <= (anchor + col[:1, :])
    systems = []
    for h in range(heads):
        spread = cols[:, h : h + 1] - running[h : h + 1, :]
        decay = jnp.where(strict, jnp.exp(spread), 0.0)
        weight = beta[h : h + 1, :] * inv[h // repeat]
        systems.append((decay * grams[h // repeat] * weight).astype(F32))
    differ = row ^ col
    inverse = [jnp.where(row == col, 1.0, 0.0) - jnp.where(differ == 1, n, 0.0) for n in systems]
    level = 1
    while (1 << level) < length:
        mask = (differ >> level) == 1
        short = [x.astype(BF16) for x in inverse]
        inner = [
            dot(jnp.where(mask, n, 0.0).astype(BF16), x).astype(BF16) for n, x in zip(systems, short)
        ]
        inverse = [x - dot(s, y) for x, s, y in zip(inverse, short, inner)]
        level += 1
    keys_t = [k.astype(F32).T for k in keys]
    for h in range(heads):
        x = inverse[h].astype(BF16)
        x_ref[h] = x
        u = dot(x, v_ref[:, h * DV : (h + 1) * DV]).astype(BF16)
        u_ref[h] = u
        tail = jnp.exp(running[h : h + 1, length - 1 : length] - running[h : h + 1, :])
        tail = jnp.where(tail_same, tail, 0.0) * beta[h : h + 1, :] * inv[h // repeat]
        a = dot((keys_t[h // repeat] * tail).astype(BF16), u)
        a_ref[h] = a
        send_ref[h] = a.astype(BF16)


def query_kernel(
    anchor_ref, doc_ref, beta_ref, gate_ref, q_ref, k_ref, z_ref, w_ref, x_ref, u_ref, m_ref, local_ref, reach_ref, gz_ref
):
    length = k_ref.shape[0]
    heads = beta_ref.shape[0]
    key_heads = k_ref.shape[1] // DK
    repeat = heads // key_heads
    anchor = anchor_ref[0]
    row, col = places(length)
    beta = jax.nn.sigmoid(beta_ref[...])
    running = prefix_sums(gate_ref[...])
    doc = doc_ref[...]
    keys = [k_ref[:, g * DK : (g + 1) * DK] for g in range(key_heads)]
    queries = [q_ref[:, g * DK : (g + 1) * DK] for g in range(key_heads)]
    inv = [lax.rsqrt(diagonal_row(dot_t(k, k), row == col) + EPS) for k in keys]
    log_q = [-0.5 * jnp.log(diagonal_row(dot_t(q, q), row == col) + EPS) for q in queries]
    log_rows = jnp.concatenate([log_q[h // repeat] for h in range(heads)], axis=0)
    alive = doc < (anchor + col[:1, :])
    alive = doc < anchor
    cols = columns_of(
        jnp.concatenate([running + log_rows, jnp.broadcast_to(doc.astype(F32), (8, length))], axis=0)
    )
    doc_col = cols[:, heads : heads + 1]
    place = (anchor + col).astype(F32)
    same = (doc_col <= place) & (col <= row)
    alive_col = doc_col < anchor.astype(F32)
    tail_same = doc[:, length - 1 : length] <= (anchor + col[:1, :])
    cross = [dot_t(q, k) for q, k in zip(queries, keys)]
    keys_t = [k.astype(F32).T for k in keys]
    for h in range(heads):
        g = h // repeat
        run = running[h : h + 1, :]
        entry = jnp.where(alive, jnp.exp(run), 0.0)
        w = dot((x_ref[h].astype(F32) * (entry * inv[g])).astype(BF16), keys[g]).astype(BF16)
        weight = beta[h : h + 1, :] * inv[g]
        decay = jnp.where(same, jnp.exp(cols[:, h : h + 1] - run), 0.0)
        scores = (decay * cross[g] * weight).astype(BF16)
        local_ref[h] = dot(scores, u_ref[h])
        lead = jnp.where(alive_col, jnp.exp(cols[:, h : h + 1]), 0.0)
        reach_ref[h] = (lead * queries[g].astype(F32) - dot(scores, w)).astype(BF16)
        tail = jnp.exp(run[:, length - 1 : length] - run)
        tail = jnp.where(tail_same, tail, 0.0) * weight
        carried = dot((keys_t[g] * tail).astype(BF16), w)
        m_ref[h] = (jnp.where(row == col, entry[:, length - 1 : length], 0.0) - carried).astype(BF16)
    z = z_ref[...].astype(F32)
    gain = z / (1.0 + jnp.exp(-z))
    for h in range(heads):
        gz_ref[h] = gain[:, h * DV : (h + 1) * DV] * w_ref[...]


def combine_kernel(s_ref, m_ref, a_ref, out_ref):
    for h in range(s_ref.shape[0]):
        out_ref[h] = (dot(m_ref[h], s_ref[h]) + a_ref[h]).astype(BF16)


def output_kernel(count, *refs):
    states = refs[:count]
    local_ref, reach_ref, gz_ref, out_ref = refs[count:]
    for h in range(local_ref.shape[0]):
        state = states[0][h]
        for other in states[1:]:
            state = state + other[h]
        mixed = local_ref[h] + dot(reach_ref[h], state)
        factor = lax.rsqrt(jnp.mean(mixed * mixed, axis=-1, keepdims=True) + EPS)
        out_ref[:, h * DV : (h + 1) * DV] = (mixed * factor * gz_ref[h]).astype(BF16)


def attention_kernel(span, window, anchor_ref, doc_ref, q_ref, gate_ref, k_ref, v_ref, out_ref):
    length = q_ref.shape[0]
    heads = q_ref.shape[1] // HD_A
    anchor = anchor_ref[0]
    total_keys = k_ref.shape[0]
    begin = jnp.clip(anchor + length - span, 0, total_keys - span)
    begin = pl.multiple_of(begin, length)
    keys = k_ref[pl.ds(begin, span), :]
    values = v_ref[pl.ds(begin, span), :]
    docs = jnp.broadcast_to(doc_ref[...].astype(F32), (length, length)).T[:, :1].astype(jnp.int32)
    q_place = anchor + lax.broadcasted_iota(jnp.int32, (length, 1), 0)
    lower = jnp.maximum(docs, q_place - window + 1)
    k_place = begin + lax.broadcasted_iota(jnp.int32, (length, span), 1)
    visible = (k_place >= lower) & (k_place <= q_place)
    for h in range(heads):
        part = slice(h * HD_A, (h + 1) * HD_A)
        scores = dot_t(q_ref[:, part], keys) * (HD_A**-0.5)
        scores = jnp.where(visible, scores, -jnp.inf)
        peak = jnp.max(scores, axis=-1, keepdims=True)
        weights = jnp.exp(scores - peak)
        total = jnp.sum(weights, axis=-1, keepdims=True)
        mixed = dot(weights.astype(BF16), values) / total
        out_ref[:, part] = (mixed * jax.nn.sigmoid(gate_ref[:, part].astype(F32))).astype(BF16)


def call(kernel, out_shape, operands, flops, scalars=1):
    moved = sum(o.size * o.dtype.itemsize for o in operands)
    specs = [pl.BlockSpec(memory_space=pltpu.SMEM)] * scalars
    specs += [pl.BlockSpec(memory_space=pltpu.VMEM)] * (len(operands) - scalars)
    return pl.pallas_call(
        kernel,
        out_shape=out_shape,
        in_specs=specs,
        out_specs=jax.tree.map(lambda _: pl.BlockSpec(memory_space=pltpu.VMEM), out_shape),
        compiler_params=pltpu.CompilerParams(vmem_limit_bytes=VMEM_LIMIT),
        cost_estimate=pl.CostEstimate(flops=flops, bytes_accessed=moved, transcendentals=0),
    )(*operands)


def shards(
    doc_start,
    q_gdn,
    k_gdn,
    v_gdn,
    z_gdn,
    beta_logit,
    log_decay,
    norm_weight,
    q_attn,
    k_attn,
    v_attn,
    gate_attn,
):
    devices = lax.axis_size("seq")
    length = q_gdn.shape[0]
    heads = v_gdn.shape[1] // DV
    place = lax.axis_index("seq").astype(jnp.int32)
    anchor = (place * length).reshape(1)
    docs = doc_start.reshape(1, length)
    shape = jax.ShapeDtypeStruct

    local_heads = q_attn.shape[1] // HD_A
    group = QH // KVH
    kv_head = lax.axis_index("head") * local_heads // group
    keys_own = lax.dynamic_slice_in_dim(k_attn, kv_head * HD_A, HD_A, 1)
    values_own = lax.dynamic_slice_in_dim(v_attn, kv_head * HD_A, HD_A, 1)
    keys_all = lax.all_gather(keys_own, "seq", axis=0, tiled=True)
    values_all = lax.all_gather(values_own, "seq", axis=0, tiled=True)

    square = (heads, length, length)
    inverse, fresh, added, leaving = call(
        state_kernel,
        (
            shape(square, BF16),
            shape((heads, length, DV), BF16),
            shape((heads, DK, DV), F32),
            shape((heads, DK, DV), BF16),
        ),
        (anchor, docs, beta_logit, log_decay, k_gdn, v_gdn),
        100 * heads * length * DK * DV,
    )
    carry, local_out, reach, gain = call(
        query_kernel,
        (
            shape((heads, DK, DK), BF16),
            shape((heads, length, DV), F32),
            shape((heads, length, DK), BF16),
            shape((heads, length, DV), F32),
        ),
        (anchor, docs, beta_logit, log_decay, q_gdn, k_gdn, z_gdn, norm_weight.reshape(1, DV), inverse, fresh),
        100 * heads * length * DK * DV,
    )
    arrived = []
    for hop in range(devices - 1):
        if hop > 0:
            leaving = call(
                combine_kernel, shape((heads, DK, DV), BF16), (arrived[-1], carry, added), 2 * heads * DK * DK * DV, 0
            )
        arrived.append(lax.ppermute(leaving, "seq", [(hop, hop + 1)]))

    shards_seen = devices // 2 + 1
    span = min(devices, shards_seen + 1) * length
    attn_out = call(
        functools.partial(attention_kernel, span, shards_seen * length),
        shape(q_attn.shape, BF16),
        (anchor, docs, q_attn, gate_attn, keys_all, values_all),
        4 * local_heads * length * span * HD_A,
    )
    gdn_out = call(
        functools.partial(output_kernel, len(arrived)),
        shape(v_gdn.shape, BF16),
        (*arrived, local_out, reach, gain),
        2 * heads * length * DK * DV,
        0,
    )
    return (gdn_out, attn_out)


def solution(mesh):
    tokens = P(("groups", "seq"))
    both = P(("groups", "seq"), "head")
    return jax.shard_map(
        shards,
        mesh=mesh,
        in_specs=(
            tokens,
            both,
            both,
            both,
            both,
            P("head", ("groups", "seq")),
            P("head", ("groups", "seq")),
            P(),
            both,
            P(("groups", "seq"), None),
            P(("groups", "seq"), None),
            both,
        ),
        out_specs=(both, both),
        check_vma=False,
    )
```

```python
import functools

import jax
import jax.numpy as jnp
from jax import lax
from jax.experimental import pallas as pl
from jax.experimental.pallas import tpu as pltpu
from jax.sharding import PartitionSpec as P

DK = 128
DV = 128
QH = 16
KVH = 2
HD_A = 256
EPS = 1e-06
VMEM_LIMIT = 48 * 1024 * 1024
PIECES = 2

F32 = jnp.float32
BF16 = jnp.bfloat16


def dot(a, b):
    return jnp.dot(a, b, preferred_element_type=F32)


def dot_t(a, b):
    return lax.dot_general(a, b, (((1,), (1,)), ((), ())), preferred_element_type=F32)


def prefix_sums(rows):
    count, length = rows.shape
    first = rows.astype(BF16)
    rest = rows - first.astype(F32)
    second = rest.astype(BF16)
    third = (rest - second.astype(F32)).astype(BF16)
    t_at = lax.broadcasted_iota(jnp.int32, (length, length), 0)
    i_at = lax.broadcasted_iota(jnp.int32, (length, length), 1)
    ones = (t_at <= i_at).astype(F32).astype(BF16)
    return dot(first, ones) + dot(second, ones) + dot(third, ones)


def columns_of(rows):
    count, length = rows.shape
    padded = jnp.concatenate([rows, jnp.zeros((length - count, length), F32)], axis=0)
    return padded.T


def diagonal_row(square, same_place):
    return jnp.sum(jnp.where(same_place, square, 0.0), axis=0, keepdims=True)


def places(length):
    row = lax.broadcasted_iota(jnp.int32, (length, length), 0)
    col = lax.broadcasted_iota(jnp.int32, (length, length), 1)
    return row, col


def pack_kernel(scalar_ref, k_hbm, v_hbm, own_ref, part_ref, sems):
    rows = part_ref.shape[0]
    column = pl.multiple_of(scalar_ref[1], HD_A)
    begin = pl.multiple_of(scalar_ref[2], rows)
    copies = []
    for side, source in enumerate((k_hbm, v_hbm)):
        lanes = pl.ds(side * HD_A, HD_A)
        wanted = pl.ds(column, HD_A)
        copies += [
            pltpu.make_async_copy(source.at[pl.ds(begin, rows), wanted], part_ref.at[:, lanes], sems.at[2 * side]),
            pltpu.make_async_copy(source.at[:, wanted], own_ref.at[:, lanes], sems.at[2 * side + 1]),
        ]
    for copy in copies:
        copy.start()
    for copy in copies:
        copy.wait()


def state_kernel(
    scalar_ref, doc_hbm, beta_hbm, gate_hbm, k_hbm, v_hbm, u_ref, w_ref, a_ref, m_ref, *rest
):
    send_refs = rest[:-6]
    doc_ref, beta_ref, gate_ref, k_ref, v_ref, sems = rest[-6:]
    sources = [(k_hbm, k_ref), (gate_hbm, gate_ref), (beta_hbm, beta_ref), (doc_hbm, doc_ref), (v_hbm, v_ref)]
    copies = [pltpu.make_async_copy(a, b, sems.at[i]) for i, (a, b) in enumerate(sources)]
    for copy in copies:
        copy.start()
    for copy in copies[:4]:
        copy.wait()
    length = k_ref.shape[0]
    heads = beta_ref.shape[0]
    key_heads = k_ref.shape[1] // DK
    repeat = heads // key_heads
    anchor = scalar_ref[0]
    row, col = places(length)
    beta = jax.nn.sigmoid(beta_ref[...])
    running = prefix_sums(gate_ref[...])
    doc = doc_ref[...]
    keys = [k_ref[:, g * DK : (g + 1) * DK] for g in range(key_heads)]
    grams = [dot_t(k, k) for k in keys]
    squares = [diagonal_row(g, row == col) + EPS for g in grams]
    log_inv = [-0.5 * jnp.log(s) for s in squares]
    inv = [lax.rsqrt(s) for s in squares]
    log_rows = jnp.concatenate([log_inv[h // repeat] for h in range(heads)], axis=0)
    cols = columns_of(
        jnp.concatenate([running + log_rows, jnp.broadcast_to(doc.astype(F32), (8, length))], axis=0)
    )
    doc_col = cols[:, heads : heads + 1]
    place = (anchor + col).astype(F32)
    strict = (doc_col <= place) & (col < row)
    tail_same = doc[:, length - 1 : length] <= (anchor + col[:1, :])
    systems = []
    for h in range(heads):
        spread = cols[:, h : h + 1] - running[h : h + 1, :]
        decay = jnp.where(strict, jnp.exp(spread), 0.0)
        weight = beta[h : h + 1, :] * inv[h // repeat]
        systems.append(decay * grams[h // repeat] * weight)
    differ = row ^ col
    inverse = [jnp.where(row == col, 1.0, 0.0) - jnp.where(differ == 1, n, 0.0) for n in systems]
    level = 1
    while (1 << level) < length:
        mask = (differ >> level) == 1
        short = [x.astype(BF16) for x in inverse]
        inner = [
            dot(jnp.where(mask, n, 0.0).astype(BF16), x).astype(BF16) for n, x in zip(systems, short)
        ]
        inverse = [x - dot(s, y) for x, s, y in zip(inverse, short, inner)]
        level += 1
    keys_t = [k.astype(F32).T for k in keys]
    for copy in copies[4:]:
        copy.wait()
    piece = heads // len(send_refs)
    for h in range(heads):
        g = h // repeat
        run = running[h : h + 1, :]
        u = dot(inverse[h].astype(BF16), v_ref[:, h * DV : (h + 1) * DV]).astype(BF16)
        u_ref[h] = u
        tail = jnp.exp(run[:, length - 1 : length] - run)
        tail = jnp.where(tail_same, tail, 0.0) * beta[h : h + 1, :] * inv[g]
        tail_keys = (keys_t[g] * tail).astype(BF16)
        a = dot(tail_keys, u)
        a_ref[h] = a
        send_refs[h // piece][h % piece] = a.astype(BF16)
        entry = jnp.where(doc < anchor, jnp.exp(run), 0.0)
        w = dot((inverse[h] * (entry * inv[g])).astype(BF16), keys[g]).astype(BF16)
        w_ref[h] = w
        m_ref[h] = (jnp.where(row == col, entry[:, length - 1 : length], 0.0) - dot(tail_keys, w)).astype(BF16)


def query_kernel(
    scalar_ref, doc_ref, beta_ref, gate_ref, q_ref, k_ref, z_ref, gain_ref, u_ref, w_ref, local_ref, reach_ref, gz_ref
):
    length = k_ref.shape[0]
    heads = beta_ref.shape[0]
    key_heads = k_ref.shape[1] // DK
    repeat = heads // key_heads
    anchor = scalar_ref[0]
    row, col = places(length)
    beta = jax.nn.sigmoid(beta_ref[...])
    running = prefix_sums(gate_ref[...])
    doc = doc_ref[...]
    keys = [k_ref[:, g * DK : (g + 1) * DK] for g in range(key_heads)]
    queries = [q_ref[:, g * DK : (g + 1) * DK] for g in range(key_heads)]
    inv = [lax.rsqrt(diagonal_row(dot_t(k, k), row == col) + EPS) for k in keys]
    log_q = [-0.5 * jnp.log(diagonal_row(dot_t(q, q), row == col) + EPS) for q in queries]
    log_rows = jnp.concatenate([log_q[h // repeat] for h in range(heads)], axis=0)
    cols = columns_of(
        jnp.concatenate([running + log_rows, jnp.broadcast_to(doc.astype(F32), (8, length))], axis=0)
    )
    doc_col = cols[:, heads : heads + 1]
    place = (anchor + col).astype(F32)
    same = (doc_col <= place) & (col <= row)
    alive_col = doc_col < anchor.astype(F32)
    cross = [dot_t(q, k) for q, k in zip(queries, keys)]
    for h in range(heads):
        g = h // repeat
        weight = beta[h : h + 1, :] * inv[g]
        decay = jnp.where(same, jnp.exp(cols[:, h : h + 1] - running[h : h + 1, :]), 0.0)
        scores = (decay * cross[g] * weight).astype(BF16)
        local_ref[h] = dot(scores, u_ref[h])
        lead = jnp.where(alive_col, jnp.exp(cols[:, h : h + 1]), 0.0)
        reach_ref[h] = (lead * queries[g].astype(F32) - dot(scores, w_ref[h])).astype(BF16)
    z = z_ref[...].astype(F32)
    gate = z / (1.0 + jnp.exp(-z))
    for h in range(heads):
        gz_ref[h] = gate[:, h * DV : (h + 1) * DV] * gain_ref[...]


def combine_kernel(begin, s_ref, m_ref, a_ref, out_ref):
    for h in range(s_ref.shape[0]):
        out_ref[h] = (dot(m_ref[begin + h], s_ref[h]) + a_ref[begin + h]).astype(BF16)


def output_kernel(hops, pieces, *refs):
    states = refs[: hops * pieces]
    local_ref, reach_ref, gz_ref, out_ref = refs[hops * pieces :]
    heads = local_ref.shape[0]
    piece = heads // pieces
    for h in range(heads):
        parts = [states[hop * pieces + h // piece][h % piece] for hop in range(hops)]
        state = parts[0]
        for other in parts[1:]:
            state = state + other
        mixed = local_ref[h] + dot(reach_ref[h], state)
        factor = lax.rsqrt(jnp.mean(mixed * mixed, axis=-1, keepdims=True) + EPS)
        out_ref[:, h * DV : (h + 1) * DV] = (mixed * factor * gz_ref[h]).astype(BF16)


def attention_kernel(window, layout, scalar_ref, doc_ref, q_ref, gate_ref, own_ref, *refs):
    sections, out_ref = refs[:-1], refs[-1]
    length = q_ref.shape[0]
    heads = q_ref.shape[1] // HD_A
    anchor = scalar_ref[0]
    docs = columns_of(jnp.broadcast_to(doc_ref[...].astype(F32), (8, length)))[:, :1].astype(jnp.int32)
    q_place = anchor + lax.broadcasted_iota(jnp.int32, (length, 1), 0)
    lower = jnp.maximum(jnp.maximum(docs, q_place - window + 1), 0)
    spots = [anchor + lax.broadcasted_iota(jnp.int32, (length, length), 1)]
    for distance, turn, rows in layout:
        start = anchor - distance * length + scalar_ref[2 + turn]
        spots.append(start + lax.broadcasted_iota(jnp.int32, (length, rows), 1))
    k_place = jnp.concatenate(spots, axis=1)
    visible = (k_place >= lower) & (k_place <= q_place)
    blocks = [own_ref, *sections]
    keys = jnp.concatenate([b[:, :HD_A] for b in blocks], axis=0)
    values = jnp.concatenate([b[:, HD_A:] for b in blocks], axis=0)
    for h in range(heads):
        part = slice(h * HD_A, (h + 1) * HD_A)
        scores = dot_t(q_ref[:, part], keys) * (HD_A**-0.5)
        scores = jnp.where(visible, scores, -jnp.inf)
        peak = jnp.max(scores, axis=-1, keepdims=True)
        weights = jnp.exp(scores - peak)
        total = jnp.sum(weights, axis=-1, keepdims=True)
        mixed = dot(weights.astype(BF16), values) / total
        out_ref[:, part] = (mixed * jax.nn.sigmoid(gate_ref[:, part].astype(F32))).astype(BF16)


def call(kernel, out_shape, operands, flops, scalars=1, outside=0, scratch=()):
    moved = sum(o.size * o.dtype.itemsize for o in operands)
    specs = [pl.BlockSpec(memory_space=pltpu.SMEM)] * scalars
    specs += [pl.BlockSpec(memory_space=pltpu.HBM)] * outside
    specs += [pl.BlockSpec(memory_space=pltpu.VMEM)] * (len(operands) - scalars - outside)
    return pl.pallas_call(
        kernel,
        out_shape=out_shape,
        in_specs=specs,
        out_specs=jax.tree.map(lambda _: pl.BlockSpec(memory_space=pltpu.VMEM), out_shape),
        scratch_shapes=scratch,
        compiler_params=pltpu.CompilerParams(vmem_limit_bytes=VMEM_LIMIT),
        cost_estimate=pl.CostEstimate(flops=flops, bytes_accessed=moved, transcendentals=0),
    )(*operands)


def after(value, *others):
    return lax.optimization_barrier((value, *others))[0]


def shards(
    doc_start,
    q_gdn,
    k_gdn,
    v_gdn,
    z_gdn,
    beta_logit,
    log_decay,
    norm_weight,
    q_attn,
    k_attn,
    v_attn,
    gate_attn,
):
    devices = lax.axis_size("seq")
    length = q_gdn.shape[0]
    heads = v_gdn.shape[1] // DV
    local_heads = q_attn.shape[1] // HD_A
    group = QH // KVH
    head_devices = lax.axis_size("head")
    sharers = max(1, min(group // local_heads, head_devices))
    rows = length // sharers
    place = lax.axis_index("seq").astype(jnp.int32)
    head_at = lax.axis_index("head").astype(jnp.int32)
    kv_head = head_at * local_heads // group
    share = head_at % sharers
    scalars = jnp.stack(
        [place * length, kv_head * HD_A] + [(share + sharers - t) % sharers * rows for t in range(sharers)]
    )
    docs = doc_start.reshape(1, length)
    shape = jax.ShapeDtypeStruct
    pieces = PIECES if heads % PIECES == 0 else 1

    own, part = call(
        pack_kernel,
        (shape((length, 2 * HD_A), BF16), shape((rows, 2 * HD_A), BF16)),
        (scalars, k_attn, v_attn),
        0,
        outside=2,
        scratch=[pltpu.SemaphoreType.DMA((4,))],
    )
    fresh, erased, added, carry, *leaving = call(
        state_kernel,
        (
            shape((heads, length, DV), BF16),
            shape((heads, length, DK), BF16),
            shape((heads, DK, DV), F32),
            shape((heads, DK, DK), BF16),
            *[shape((heads // pieces, DK, DV), BF16)] * pieces,
        ),
        (scalars, docs, beta_logit, log_decay, k_gdn, v_gdn),
        100 * heads * length * DK * DV,
        outside=5,
        scratch=[
            pltpu.VMEM(docs.shape, jnp.int32),
            pltpu.VMEM(beta_logit.shape, F32),
            pltpu.VMEM(log_decay.shape, F32),
            pltpu.VMEM(k_gdn.shape, BF16),
            pltpu.VMEM(v_gdn.shape, BF16),
            pltpu.SemaphoreType.DMA((5,)),
        ],
    )

    wanted = min(devices // 2 + 1, devices - 1)
    units = [part]
    layout = []
    sections = []
    have = 1
    while have < wanted + 1:
        take = min(have, wanted + 1 - have)
        block = units[0] if take == 1 else jnp.concatenate(units[:take], axis=0)
        got = lax.ppermute(block, "seq", [(i, i + have) for i in range(devices - have)])
        for turn in range(sharers):
            if turn == 0:
                swapped = got
            else:
                swapped = lax.ppermute(
                    got, "head", [(i, i // sharers * sharers + (i + turn) % sharers) for i in range(head_devices)]
                )
            for step in range(take):
                layout.append((have + step, turn, rows))
                sections.append(swapped[step * rows : (step + 1) * rows])
        units += [got[step * rows : (step + 1) * rows] for step in range(take)]
        have += take

    arrived = [[lax.ppermute(s, "seq", [(0, 1)]) for s in leaving]]
    local_out, reach, gain = call(
        query_kernel,
        (
            shape((heads, length, DV), F32),
            shape((heads, length, DK), BF16),
            shape((heads, length, DV), F32),
        ),
        (scalars, docs, beta_logit, log_decay, q_gdn, k_gdn, z_gdn, norm_weight.reshape(1, DV), fresh, erased),
        100 * heads * length * DK * DV,
    )
    piece = heads // pieces
    for hop in range(1, devices - 1):
        leaving = [
            call(
                functools.partial(combine_kernel, at * piece),
                shape((piece, DK, DV), BF16),
                (arrived[-1][at], carry, added),
                2 * piece * DK * DK * DV,
                0,
            )
            for at in range(pieces)
        ]
        arrived.append([lax.ppermute(s, "seq", [(hop, hop + 1)]) for s in leaving])

    attn_out = call(
        functools.partial(attention_kernel, (devices // 2 + 1) * length, layout),
        shape(q_attn.shape, BF16),
        (scalars, docs, q_attn, gate_attn, own, *sections),
        4 * local_heads * length * length * (wanted + 1) * HD_A,
    )
    gdn_out = call(
        functools.partial(output_kernel, len(arrived), pieces),
        shape(v_gdn.shape, BF16),
        (*[s for hop in arrived for s in hop], local_out, reach, gain),
        2 * heads * length * DK * DV,
        0,
    )
    return (gdn_out, attn_out)


def solution(mesh):
    tokens = P(("groups", "seq"))
    both = P(("groups", "seq"), "head")
    return jax.shard_map(
        shards,
        mesh=mesh,
        in_specs=(
            tokens,
            both,
            both,
            both,
            both,
            P("head", ("groups", "seq")),
            P("head", ("groups", "seq")),
            P(),
            both,
            P(("groups", "seq"), None),
            P(("groups", "seq"), None),
            both,
        ),
        out_specs=(both, both),
        check_vma=False,
    )
```

```python
import functools

import jax
import jax.numpy as jnp
from jax import lax
from jax.experimental import pallas as pl
from jax.experimental.pallas import tpu as pltpu
from jax.sharding import PartitionSpec as P

DK = 128
DV = 128
QH = 16
KVH = 2
HD_A = 256
EPS = 1e-06
VMEM_LIMIT = 48 * 1024 * 1024
PIECES = 2

F32 = jnp.float32
BF16 = jnp.bfloat16


def dot(a, b):
    return jnp.dot(a, b, preferred_element_type=F32)


def dot_t(a, b):
    return lax.dot_general(a, b, (((1,), (1,)), ((), ())), preferred_element_type=F32)


def prefix_sums(rows):
    count, length = rows.shape
    first = rows.astype(BF16)
    rest = rows - first.astype(F32)
    second = rest.astype(BF16)
    third = (rest - second.astype(F32)).astype(BF16)
    t_at = lax.broadcasted_iota(jnp.int32, (length, length), 0)
    i_at = lax.broadcasted_iota(jnp.int32, (length, length), 1)
    ones = (t_at <= i_at).astype(F32).astype(BF16)
    return dot(first, ones) + dot(second, ones) + dot(third, ones)


def columns_of(rows):
    count, length = rows.shape
    padded = jnp.concatenate([rows, jnp.zeros((length - count, length), F32)], axis=0)
    return padded.T


def diagonal_row(square, same_place):
    return jnp.sum(jnp.where(same_place, square, 0.0), axis=0, keepdims=True)


def places(length):
    row = lax.broadcasted_iota(jnp.int32, (length, length), 0)
    col = lax.broadcasted_iota(jnp.int32, (length, length), 1)
    return row, col


def state_terms(scalar_ref, inputs, u_ref, w_ref=None, a_ref=None, m_ref=None, send_refs=()):
    k_ref, gate_ref, beta_ref, doc_ref, v_ref = inputs
    doc = doc_ref[...]
    anchor = scalar_ref[0]
    length = k_ref.shape[0]
    heads = beta_ref.shape[0]
    key_heads = k_ref.shape[1] // DK
    repeat = heads // key_heads
    row, col = places(length)
    beta = jax.nn.sigmoid(beta_ref[...])
    running = prefix_sums(gate_ref[...])
    keys = [k_ref[:, g * DK : (g + 1) * DK] for g in range(key_heads)]
    grams = [dot_t(k, k) for k in keys]
    squares = [diagonal_row(g, row == col) + EPS for g in grams]
    log_inv = [-0.5 * jnp.log(s) for s in squares]
    inv = [lax.rsqrt(s) for s in squares]
    log_rows = jnp.concatenate([log_inv[h // repeat] for h in range(heads)], axis=0)
    cols = columns_of(
        jnp.concatenate([running + log_rows, jnp.broadcast_to(doc.astype(F32), (8, length))], axis=0)
    )
    doc_col = cols[:, heads : heads + 1]
    place = (anchor + col).astype(F32)
    strict = (doc_col <= place) & (col < row)
    tail_same = doc[:, length - 1 : length] <= (anchor + col[:1, :])
    systems = []
    for h in range(heads):
        spread = cols[:, h : h + 1] - running[h : h + 1, :]
        decay = jnp.where(strict, jnp.exp(spread), 0.0)
        weight = beta[h : h + 1, :] * inv[h // repeat]
        systems.append(decay * grams[h // repeat] * weight)
    differ = row ^ col
    inverse = [jnp.where(row == col, 1.0, 0.0) - jnp.where(differ == 1, n, 0.0) for n in systems]
    level = 1
    while (1 << level) < length:
        mask = (differ >> level) == 1
        short = [x.astype(BF16) for x in inverse]
        inner = [
            dot(jnp.where(mask, n, 0.0).astype(BF16), x).astype(BF16) for n, x in zip(systems, short)
        ]
        inverse = [x - dot(s, y) for x, s, y in zip(inverse, short, inner)]
        level += 1
    keys_t = [k.astype(F32).T for k in keys]
    for h in range(heads):
        g = h // repeat
        run = running[h : h + 1, :]
        u = dot(inverse[h].astype(BF16), v_ref[:, h * DV : (h + 1) * DV]).astype(BF16)
        u_ref[h] = u
        tail = jnp.exp(run[:, length - 1 : length] - run)
        tail = jnp.where(tail_same, tail, 0.0) * beta[h : h + 1, :] * inv[g]
        tail_keys = (keys_t[g] * tail).astype(BF16)
        a = dot(tail_keys, u)
        if send_refs:
            piece = heads // len(send_refs)
            send_refs[h // piece][h % piece] = a.astype(BF16)
            continue
        a_ref[h] = a
        entry = jnp.where(doc < anchor, jnp.exp(run), 0.0)
        w = dot((inverse[h] * (entry * inv[g])).astype(BF16), keys[g]).astype(BF16)
        w_ref[h] = w
        m_ref[h] = (jnp.where(row == col, entry[:, length - 1 : length], 0.0) - dot(tail_keys, w)).astype(BF16)


def opening_kernel(scalar_ref, *refs):
    sources, (ka_hbm, va_hbm) = refs[:6], refs[6:8]
    inputs, (unit_ref, u_ref), send_refs, sems = refs[8:14], refs[14:16], refs[16:-1], refs[-1]
    groups = HD_A // DK
    rows = unit_ref.shape[0] // (2 * groups)
    column = pl.multiple_of(scalar_ref[1], HD_A)
    begin = pl.multiple_of(scalar_ref[2], rows)
    pairs = list(zip(sources, inputs))
    for at in range(2 * groups):
        source = (ka_hbm, va_hbm)[at // groups].at[pl.ds(begin, rows), pl.ds(column + at % groups * DK, DK)]
        pairs.append((source, unit_ref.at[pl.ds(at * rows, rows)]))
    copies = [pltpu.make_async_copy(a, b, sems.at[i]) for i, (a, b) in enumerate(pairs)]
    for copy in copies:
        copy.start()
    for copy in copies:
        copy.wait()

    @pl.when(scalar_ref[0] == 0)
    def _():
        state_terms(scalar_ref, inputs[:5], u_ref, send_refs=send_refs)


def second_kernel(scalar_ref, *refs):
    inputs, (_, u_ref, w_ref, a_ref, m_ref) = refs[:5], refs[5:]
    length = u_ref.shape[1]

    @pl.when(scalar_ref[0] == 0)
    def _():
        w_ref[...] = jnp.zeros(w_ref.shape, BF16)

    @pl.when(scalar_ref[0] == length)
    def _():
        state_terms(scalar_ref, inputs, u_ref, w_ref, a_ref, m_ref)


def later_kernel(scalar_ref, *refs):
    inputs, outs = refs[:5], refs[9:]
    length = outs[0].shape[1]

    @pl.when(scalar_ref[0] > length)
    def _():
        state_terms(scalar_ref, inputs, *outs)


def query_kernel(
    scalar_ref, doc_ref, beta_ref, gate_ref, q_ref, k_ref, z_ref, gain_ref, u_ref, w_ref, local_ref, reach_ref, gz_ref
):
    length = k_ref.shape[0]
    heads = beta_ref.shape[0]
    key_heads = k_ref.shape[1] // DK
    repeat = heads // key_heads
    anchor = scalar_ref[0]
    row, col = places(length)
    beta = jax.nn.sigmoid(beta_ref[...])
    running = prefix_sums(gate_ref[...])
    doc = doc_ref[...]
    keys = [k_ref[:, g * DK : (g + 1) * DK] for g in range(key_heads)]
    queries = [q_ref[:, g * DK : (g + 1) * DK] for g in range(key_heads)]
    inv = [lax.rsqrt(diagonal_row(dot_t(k, k), row == col) + EPS) for k in keys]
    log_q = [-0.5 * jnp.log(diagonal_row(dot_t(q, q), row == col) + EPS) for q in queries]
    log_rows = jnp.concatenate([log_q[h // repeat] for h in range(heads)], axis=0)
    cols = columns_of(
        jnp.concatenate([running + log_rows, jnp.broadcast_to(doc.astype(F32), (8, length))], axis=0)
    )
    doc_col = cols[:, heads : heads + 1]
    place = (anchor + col).astype(F32)
    same = (doc_col <= place) & (col <= row)
    alive_col = doc_col < anchor.astype(F32)
    cross = [dot_t(q, k) for q, k in zip(queries, keys)]
    for h in range(heads):
        g = h // repeat
        weight = beta[h : h + 1, :] * inv[g]
        decay = jnp.where(same, jnp.exp(cols[:, h : h + 1] - running[h : h + 1, :]), 0.0)
        scores = (decay * cross[g] * weight).astype(BF16)
        local_ref[h] = dot(scores, u_ref[h])
        lead = jnp.where(alive_col, jnp.exp(cols[:, h : h + 1]), 0.0)
        reach_ref[h] = (lead * queries[g].astype(F32) - dot(scores, w_ref[h])).astype(BF16)
    z = z_ref[...].astype(F32)
    gate = z / (1.0 + jnp.exp(-z))
    for h in range(heads):
        gz_ref[h] = gate[:, h * DV : (h + 1) * DV] * gain_ref[...]


def combine_kernel(begin, s_ref, m_ref, a_ref, out_ref):
    for h in range(s_ref.shape[0]):
        out_ref[h] = (dot(m_ref[begin + h], s_ref[h]) + a_ref[begin + h]).astype(BF16)


def normed_piece(begin, states, local_ref, reach_ref, gz_ref, out_ref, columns):
    for at in range(states[0].shape[0]):
        state = states[0][at]
        for other in states[1:]:
            state = state + other[at]
        h = begin + at
        mixed = local_ref[h] + dot(reach_ref[h], state)
        factor = lax.rsqrt(jnp.mean(mixed * mixed, axis=-1, keepdims=True) + EPS)
        spot = columns + at * DV
        out_ref[:, spot : spot + DV] = (mixed * factor * gz_ref[h]).astype(BF16)


def piece_kernel(begin, hops, *refs):
    normed_piece(begin, refs[:hops], *refs[hops:], 0)


def output_kernel(begin, hops, *refs):
    states, terms, ready = refs[:hops], refs[hops : hops + 3], refs[hops + 3 : -3]
    out_hbm, held_ref, sems = refs[-3:]
    copies = []
    spot = 0
    for at, part in enumerate((*ready, held_ref)):
        if part is held_ref:
            normed_piece(begin, states, *terms, held_ref, 0)
        width = part.shape[1]
        copies.append(pltpu.make_async_copy(part, out_hbm.at[:, spot : spot + width], sems.at[at]))
        copies[-1].start()
        spot += width
    for copy in copies:
        copy.wait()


def attention_kernel(window, layout, scalar_ref, doc_ref, q_ref, gate_ref, k_ref, v_ref, *refs):
    units, (out_hbm, held_ref, sems) = refs[:-3], refs[-3:]
    length = q_ref.shape[0]
    heads = q_ref.shape[1] // HD_A
    groups = HD_A // DK
    anchor = scalar_ref[0]
    docs = columns_of(jnp.broadcast_to(doc_ref[...].astype(F32), (8, length)))[:, :1].astype(jnp.int32)
    q_place = anchor + lax.broadcasted_iota(jnp.int32, (length, 1), 0)
    lower = jnp.maximum(jnp.maximum(docs, q_place - window + 1), 0)
    spots = [anchor + lax.broadcasted_iota(jnp.int32, (length, length), 1)]
    wanted = pl.ds(pl.multiple_of(scalar_ref[1], HD_A), HD_A)
    keys, values = [k_ref[:, wanted]], [v_ref[:, wanted]]
    for (distance, turn), unit in zip(layout, units):
        rows = unit.shape[0] // (2 * groups)
        start = anchor - distance * length + scalar_ref[2 + turn]
        spots.append(start + lax.broadcasted_iota(jnp.int32, (length, rows), 1))
        blocks = [unit[at * rows : (at + 1) * rows] for at in range(2 * groups)]
        keys.append(jnp.concatenate(blocks[:groups], axis=1))
        values.append(jnp.concatenate(blocks[groups:], axis=1))
    k_place = jnp.concatenate(spots, axis=1)
    visible = (k_place >= lower) & (k_place <= q_place)
    keys = jnp.concatenate(keys, axis=0)
    values = jnp.concatenate(values, axis=0)
    step = 2
    copies = []
    for first in range(0, heads, step):
        names = range(first, min(first + step, heads))
        queries = jnp.concatenate([q_ref[:, h * HD_A : (h + 1) * HD_A] for h in names], axis=0)
        scores = dot_t(queries * BF16(HD_A**-0.5), keys)
        scores = jnp.where(jnp.concatenate([visible] * len(names), axis=0), scores, -jnp.inf)
        peak = jnp.max(scores, axis=-1, keepdims=True)
        weights = jnp.exp(scores - peak)
        total = jnp.sum(weights, axis=-1, keepdims=True)
        mixed = dot(weights.astype(BF16), values)
        for at, h in enumerate(names):
            part = slice(h * HD_A, (h + 1) * HD_A)
            rows = slice(at * length, (at + 1) * length)
            gate = 1.0 + jnp.exp(-gate_ref[:, part].astype(F32))
            held_ref[:, part] = (mixed[rows] / (total[rows] * gate)).astype(BF16)
            copy = pltpu.make_async_copy(held_ref.at[:, part], out_hbm.at[:, part], sems.at[h])
            copy.start()
            copies.append(copy)
    for copy in copies:
        copy.wait()


def call(kernel, out_shape, operands, flops, scalars=1, outside=0, scratch=(), aliases=None, held=pltpu.VMEM):
    moved = sum(o.size * o.dtype.itemsize for o in operands)
    inside = len(operands) - scalars - outside
    operands = [
        pltpu.with_memory_space_constraint(o, pltpu.HBM) if scalars <= i < scalars + outside else o
        for i, o in enumerate(operands)
    ]
    specs = [pl.BlockSpec(memory_space=pltpu.SMEM)] * scalars
    specs += [pl.BlockSpec(memory_space=pltpu.HBM)] * outside
    specs += [pl.BlockSpec(memory_space=pltpu.VMEM)] * inside
    if held is not pltpu.VMEM and aliases:
        specs[-1] = pl.BlockSpec(memory_space=held)
    return pl.pallas_call(
        kernel,
        out_shape=out_shape,
        in_specs=specs,
        out_specs=jax.tree.map(lambda _: pl.BlockSpec(memory_space=held), out_shape),
        scratch_shapes=scratch,
        input_output_aliases=aliases or {},
        compiler_params=pltpu.CompilerParams(vmem_limit_bytes=VMEM_LIMIT),
        cost_estimate=pl.CostEstimate(flops=flops, bytes_accessed=moved, transcendentals=0),
    )(*operands)


def after(value, *others):
    return lax.optimization_barrier((value, *others))[0]


def shards(
    doc_start,
    q_gdn,
    k_gdn,
    v_gdn,
    z_gdn,
    beta_logit,
    log_decay,
    norm_weight,
    q_attn,
    k_attn,
    v_attn,
    gate_attn,
):
    devices = lax.axis_size("seq")
    length = q_gdn.shape[0]
    heads = v_gdn.shape[1] // DV
    local_heads = q_attn.shape[1] // HD_A
    group = QH // KVH
    head_devices = lax.axis_size("head")
    sharers = max(1, min(group // local_heads, head_devices))
    rows = length // sharers
    place = lax.axis_index("seq").astype(jnp.int32)
    head_at = lax.axis_index("head").astype(jnp.int32)
    kv_head = head_at * local_heads // group
    share = head_at % sharers
    scalars = jnp.stack(
        [place * length, kv_head * HD_A] + [(share + sharers - t) % sharers * rows for t in range(sharers)]
    )
    docs = doc_start.reshape(1, length)
    shape = jax.ShapeDtypeStruct
    pieces = PIECES if heads % PIECES == 0 else 1

    sources = (k_gdn, log_decay, beta_logit, docs, v_gdn, norm_weight.reshape(1, DV))
    terms = (
        shape((heads, length, DV), BF16),
        shape((heads, length, DK), BF16),
        shape((heads, DK, DV), F32),
        shape((heads, DK, DK), BF16),
    )
    work = 100 * heads * length * DK * DV
    piece = heads // pieces
    groups = HD_A // DK
    opened = call(
        opening_kernel,
        (
            *[shape(a.shape, a.dtype) for a in sources],
            shape((2 * groups * rows, DK), BF16),
            terms[0],
            *[shape((piece, DK, DV), BF16)] * pieces,
        ),
        (scalars, *sources, k_attn, v_attn),
        work,
        outside=len(sources) + 2,
        scratch=[pltpu.SemaphoreType.DMA((len(sources) + 2 * groups,))],
    )
    inputs, (gain_in, unit, fresh), leaving = opened[:5], opened[5:8], opened[8:]

    def hand_on(hop, pieces_out):
        return [lax.ppermute(s, "seq", [(hop, hop + 1)]) for s in pieces_out]

    def combined(got, carry, added, between=None):
        done = []
        for at, state in enumerate(got):
            if at == 1 and between:
                state = after(state, *between(done[0]))
            elif done:
                state = after(state, done[-1])
            done.append(
                call(
                    functools.partial(combine_kernel, at * piece),
                    shape((piece, DK, DV), BF16),
                    (state, carry, added),
                    2 * piece * DK * DK * DV,
                    0,
                )
            )
        return done

    def swapped(got, turn):
        pairs = [(i, i // sharers * sharers + (i + turn) % sharers) for i in range(head_devices)]
        return lax.ppermute(got, "head", pairs)

    wanted = min(devices // 2 + 1, devices - 1)
    arrived = [hand_on(0, leaving)]
    fresh, erased, added, carry = call(
        second_kernel, terms, (scalars, *inputs, fresh), work, aliases={6: 0}
    )
    unit = after(unit, fresh)
    units = [lax.ppermute(unit, "seq", [(i, i + 1) for i in range(devices - 1)])]
    direct = wanted == devices - 1 and wanted > 1
    farthest = [lax.ppermute(unit, "seq", [(0, wanted)])] if direct else []
    leaving = combined(arrived[-1], carry, added)
    arrived.append(hand_on(1, leaving))
    block = after(units[0], leaving[-1])
    for distance in range(2, wanted + 1 - direct):
        block = lax.ppermute(block, "seq", [(i, i + 1) for i in range(distance - 1, devices - 1)])
        units.append(block)
    units += farthest
    fresh, erased, added, carry = call(
        later_kernel,
        terms,
        (scalars, *inputs, after(fresh, leaving[-1]), erased, added, carry),
        work,
        aliases={6: 0, 7: 1, 8: 2, 9: 3},
    )
    def queries(first):
        mixing.extend(call(
            query_kernel,
            (
                shape((heads, length, DV), F32),
                shape((heads, length, DK), BF16),
                shape((heads, length, DV), F32),
            ),
            (
                *(scalars, inputs[3], inputs[2], inputs[1], q_gdn, inputs[0], z_gdn, gain_in),
                *(after(fresh, first), erased),
            ),
            work,
        ))
        return mixing[:1]

    mixing = []
    for hop in range(2, devices - 1):
        leaving = combined(arrived[-1], carry, added, queries if hop == 2 else None)
        arrived.append(hand_on(hop, leaving))
    local_out, reach, gain = mixing

    layout, sections = [], []
    for distance, got in enumerate(units, 1):
        for turn in range(sharers):
            layout.append((distance, turn))
            sections.append(swapped(after(got, leaving[-1]), turn) if turn else got)
    attn_out = call(
        functools.partial(attention_kernel, (devices // 2 + 1) * length, layout),
        shape(q_attn.shape, BF16),
        (scalars, inputs[3], q_attn, gate_attn, k_attn, v_attn, *sections),
        4 * local_heads * length * length * (wanted + 1) * HD_A,
        scratch=[pltpu.VMEM(q_attn.shape, BF16), pltpu.SemaphoreType.DMA((local_heads,))],
        held=pltpu.HBM,
    )
    ready = []
    for at in range(pieces):
        states = [got[at] for got in arrived]
        operands = (*states, after(local_out, attn_out), reach, gain)
        cost = 2 * piece * length * DK * DV
        if at < pieces - 1:
            ready.append(
                call(
                    functools.partial(piece_kernel, at * piece, len(states)),
                    shape((length, piece * DV), BF16),
                    operands,
                    cost,
                    0,
                )
            )
    gdn_out = call(
        functools.partial(output_kernel, at * piece, len(states)),
        shape(v_gdn.shape, BF16),
        (*operands, *ready),
        cost,
        0,
        scratch=[pltpu.VMEM((length, piece * DV), BF16), pltpu.SemaphoreType.DMA((pieces,))],
        held=pltpu.HBM,
    )
    return (gdn_out, attn_out)


def solution(mesh):
    tokens = P(("groups", "seq"))
    both = P(("groups", "seq"), "head")
    return jax.shard_map(
        shards,
        mesh=mesh,
        in_specs=(
            tokens,
            both,
            both,
            both,
            both,
            P("head", ("groups", "seq")),
            P("head", ("groups", "seq")),
            P(),
            both,
            P(("groups", "seq"), None),
            P(("groups", "seq"), None),
            both,
        ),
        out_specs=(both, both),
        check_vma=False,
    )
```

```python
import functools

import jax
import jax.numpy as jnp
from jax import lax
from jax.experimental import pallas as pl
from jax.experimental.pallas import tpu as pltpu
from jax.sharding import PartitionSpec as P

DK = 128
DV = 128
QH = 16
KVH = 2
HD_A = 256
EPS = 1e-06
VMEM_LIMIT = 48 * 1024 * 1024
PIECES = 2

F32 = jnp.float32
BF16 = jnp.bfloat16


def dot(a, b):
    return jnp.dot(a, b, preferred_element_type=F32)


def dot_t(a, b):
    return lax.dot_general(a, b, (((1,), (1,)), ((), ())), preferred_element_type=F32)


def prefix_sums(rows):
    count, length = rows.shape
    first = rows.astype(BF16)
    rest = rows - first.astype(F32)
    second = rest.astype(BF16)
    third = (rest - second.astype(F32)).astype(BF16)
    t_at = lax.broadcasted_iota(jnp.int32, (length, length), 0)
    i_at = lax.broadcasted_iota(jnp.int32, (length, length), 1)
    ones = (t_at <= i_at).astype(F32).astype(BF16)
    return dot(first, ones) + dot(second, ones) + dot(third, ones)


def columns_of(rows):
    count, length = rows.shape
    padded = jnp.concatenate([rows, jnp.zeros((length - count, length), F32)], axis=0)
    return padded.T


def diagonal_row(square, same_place):
    return jnp.sum(jnp.where(same_place, square, 0.0), axis=0, keepdims=True)


def places(length):
    row = lax.broadcasted_iota(jnp.int32, (length, length), 0)
    col = lax.broadcasted_iota(jnp.int32, (length, length), 1)
    return row, col


def state_terms(scalar_ref, inputs, u_ref, w_ref=None, a_ref=None, m_ref=None, send_refs=()):
    k_ref, gate_ref, beta_ref, doc_ref, v_ref = inputs
    doc = doc_ref[...]
    anchor = scalar_ref[0]
    length = k_ref.shape[0]
    heads = beta_ref.shape[0]
    key_heads = k_ref.shape[1] // DK
    repeat = heads // key_heads
    row, col = places(length)
    beta = jax.nn.sigmoid(beta_ref[...])
    running = prefix_sums(gate_ref[...])
    keys = [k_ref[:, g * DK : (g + 1) * DK] for g in range(key_heads)]
    grams = [dot_t(k, k) for k in keys]
    squares = [diagonal_row(g, row == col) + EPS for g in grams]
    log_inv = [-0.5 * jnp.log(s) for s in squares]
    inv = [lax.rsqrt(s) for s in squares]
    log_rows = jnp.concatenate([log_inv[h // repeat] for h in range(heads)], axis=0)
    cols = columns_of(
        jnp.concatenate([running + log_rows, jnp.broadcast_to(doc.astype(F32), (8, length))], axis=0)
    )
    doc_col = cols[:, heads : heads + 1]
    place = (anchor + col).astype(F32)
    strict = (doc_col <= place) & (col < row)
    tail_same = doc[:, length - 1 : length] <= (anchor + col[:1, :])
    systems = []
    for h in range(heads):
        spread = cols[:, h : h + 1] - running[h : h + 1, :]
        decay = jnp.where(strict, jnp.exp(spread), 0.0)
        weight = beta[h : h + 1, :] * inv[h // repeat]
        systems.append(decay * grams[h // repeat] * weight)
    differ = row ^ col
    inverse = [jnp.where(row == col, 1.0, 0.0) - jnp.where(differ == 1, n, 0.0) for n in systems]
    level = 1
    while (1 << level) < length:
        mask = (differ >> level) == 1
        short = [x.astype(BF16) for x in inverse]
        inner = [
            dot(jnp.where(mask, n, 0.0).astype(BF16), x).astype(BF16) for n, x in zip(systems, short)
        ]
        inverse = [x - dot(s, y) for x, s, y in zip(inverse, short, inner)]
        level += 1
    keys_t = [k.astype(F32).T for k in keys]
    for h in range(heads):
        g = h // repeat
        run = running[h : h + 1, :]
        u = dot(inverse[h].astype(BF16), v_ref[:, h * DV : (h + 1) * DV]).astype(BF16)
        u_ref[h] = u
        tail = jnp.exp(run[:, length - 1 : length] - run)
        tail = jnp.where(tail_same, tail, 0.0) * beta[h : h + 1, :] * inv[g]
        tail_keys = (keys_t[g] * tail).astype(BF16)
        a = dot(tail_keys, u)
        if send_refs:
            piece = heads // len(send_refs)
            send_refs[h // piece][h % piece] = a.astype(BF16)
            continue
        a_ref[h] = a
        entry = jnp.where(doc < anchor, jnp.exp(run), 0.0)
        w = dot((inverse[h] * (entry * inv[g])).astype(BF16), keys[g]).astype(BF16)
        w_ref[h] = w
        m_ref[h] = (jnp.where(row == col, entry[:, length - 1 : length], 0.0) - dot(tail_keys, w)).astype(BF16)


def opening_kernel(scalar_ref, *refs):
    sources, u_ref, send_refs = refs[:5], refs[5], refs[6:-6]
    inputs, sems = refs[-6:-1], refs[-1]

    @pl.when(scalar_ref[0] == 0)
    def _():
        copies = [pltpu.make_async_copy(a, b, sems.at[i]) for i, (a, b) in enumerate(zip(sources, inputs))]
        for copy in copies:
            copy.start()
        for copy in copies:
            copy.wait()
        state_terms(scalar_ref, inputs, u_ref, send_refs=send_refs)


def second_kernel(scalar_ref, *refs):
    inputs, (ka_ref, va_ref, gain_ref, _) = refs[:5], refs[5:9]
    u_ref, w_ref, a_ref, m_ref, unit_ref, kept_ref = refs[9:]
    kept_ref[...] = gain_ref[...]
    length = u_ref.shape[1]
    groups = HD_A // DK
    rows = unit_ref.shape[0] // (2 * groups)
    begin = pl.multiple_of(scalar_ref[2], rows)
    for at in range(2 * groups):
        lanes = pl.ds(pl.multiple_of(scalar_ref[1] + at % groups * DK, DK), DK)
        unit_ref[at * rows : (at + 1) * rows] = (ka_ref, va_ref)[at // groups][pl.ds(begin, rows), lanes]

    @pl.when(scalar_ref[0] == 0)
    def _():
        w_ref[...] = jnp.zeros(w_ref.shape, BF16)

    @pl.when(scalar_ref[0] == length)
    def _():
        state_terms(scalar_ref, inputs, u_ref, w_ref, a_ref, m_ref)


def later_kernel(scalar_ref, *refs):
    inputs, outs = refs[:5], refs[9:]
    length = outs[0].shape[1]

    @pl.when(scalar_ref[0] > length)
    def _():
        state_terms(scalar_ref, inputs, *outs)


def query_kernel(
    scalar_ref, doc_ref, beta_ref, gate_ref, q_ref, k_ref, z_ref, gain_ref, u_ref, w_ref, local_ref, reach_ref, gz_ref
):
    length = k_ref.shape[0]
    heads = beta_ref.shape[0]
    key_heads = k_ref.shape[1] // DK
    repeat = heads // key_heads
    anchor = scalar_ref[0]
    row, col = places(length)
    beta = jax.nn.sigmoid(beta_ref[...])
    running = prefix_sums(gate_ref[...])
    doc = doc_ref[...]
    keys = [k_ref[:, g * DK : (g + 1) * DK] for g in range(key_heads)]
    queries = [q_ref[:, g * DK : (g + 1) * DK] for g in range(key_heads)]
    inv = [lax.rsqrt(diagonal_row(dot_t(k, k), row == col) + EPS) for k in keys]
    log_q = [-0.5 * jnp.log(diagonal_row(dot_t(q, q), row == col) + EPS) for q in queries]
    log_rows = jnp.concatenate([log_q[h // repeat] for h in range(heads)], axis=0)
    cols = columns_of(
        jnp.concatenate([running + log_rows, jnp.broadcast_to(doc.astype(F32), (8, length))], axis=0)
    )
    doc_col = cols[:, heads : heads + 1]
    place = (anchor + col).astype(F32)
    same = (doc_col <= place) & (col <= row)
    alive_col = doc_col < anchor.astype(F32)
    cross = [dot_t(q, k) for q, k in zip(queries, keys)]
    for h in range(heads):
        g = h // repeat
        weight = beta[h : h + 1, :] * inv[g]
        decay = jnp.where(same, jnp.exp(cols[:, h : h + 1] - running[h : h + 1, :]), 0.0)
        scores = (decay * cross[g] * weight).astype(BF16)
        local_ref[h] = dot(scores, u_ref[h])
        lead = jnp.where(alive_col, jnp.exp(cols[:, h : h + 1]), 0.0)
        reach_ref[h] = (lead * queries[g].astype(F32) - dot(scores, w_ref[h])).astype(BF16)
    z = z_ref[...].astype(F32)
    gate = z / (1.0 + jnp.exp(-z))
    for h in range(heads):
        gz_ref[h] = gate[:, h * DV : (h + 1) * DV] * gain_ref[...]


def combine_kernel(begin, s_ref, m_ref, a_ref, out_ref):
    for h in range(s_ref.shape[0]):
        out_ref[h] = (dot(m_ref[begin + h], s_ref[h]) + a_ref[begin + h]).astype(BF16)


def normed_piece(begin, states, local_ref, reach_ref, gz_ref, out_ref, columns):
    for at in range(states[0].shape[0]):
        state = states[0][at]
        for other in states[1:]:
            state = state + other[at]
        h = begin + at
        mixed = local_ref[h] + dot(reach_ref[h], state)
        factor = lax.rsqrt(jnp.mean(mixed * mixed, axis=-1, keepdims=True) + EPS)
        spot = columns + at * DV
        out_ref[:, spot : spot + DV] = (mixed * factor * gz_ref[h]).astype(BF16)


def piece_kernel(begin, hops, *refs):
    normed_piece(begin, refs[:hops], *refs[hops:], 0)


def output_kernel(begin, hops, *refs):
    states, terms, ready = refs[:hops], refs[hops : hops + 3], refs[hops + 3 : -3]
    out_hbm, held_ref, sems = refs[-3:]
    copies = []
    spot = 0
    for at, part in enumerate((*ready, held_ref)):
        if part is held_ref:
            normed_piece(begin, states, *terms, held_ref, 0)
        width = part.shape[1]
        copies.append(pltpu.make_async_copy(part, out_hbm.at[:, spot : spot + width], sems.at[at]))
        copies[-1].start()
        spot += width
    for copy in copies:
        copy.wait()


def attention_kernel(window, layout, scalar_ref, doc_ref, q_ref, gate_ref, k_ref, v_ref, *refs):
    units, (out_hbm, held_ref, sems) = refs[:-3], refs[-3:]
    length = q_ref.shape[0]
    heads = q_ref.shape[1] // HD_A
    groups = HD_A // DK
    anchor = scalar_ref[0]
    docs = columns_of(jnp.broadcast_to(doc_ref[...].astype(F32), (8, length)))[:, :1].astype(jnp.int32)
    q_place = anchor + lax.broadcasted_iota(jnp.int32, (length, 1), 0)
    lower = jnp.maximum(jnp.maximum(docs, q_place - window + 1), 0)
    spots = [anchor + lax.broadcasted_iota(jnp.int32, (length, length), 1)]
    wanted = pl.ds(pl.multiple_of(scalar_ref[1], HD_A), HD_A)
    keys, values = [k_ref[:, wanted]], [v_ref[:, wanted]]
    for (distance, turn), unit in zip(layout, units):
        rows = unit.shape[0] // (2 * groups)
        start = anchor - distance * length + scalar_ref[2 + turn]
        spots.append(start + lax.broadcasted_iota(jnp.int32, (length, rows), 1))
        blocks = [unit[at * rows : (at + 1) * rows] for at in range(2 * groups)]
        keys.append(jnp.concatenate(blocks[:groups], axis=1))
        values.append(jnp.concatenate(blocks[groups:], axis=1))
    k_place = jnp.concatenate(spots, axis=1)
    visible = (k_place >= lower) & (k_place <= q_place)
    keys = jnp.concatenate(keys, axis=0)
    values = jnp.concatenate(values, axis=0)
    step = 2
    copies = []
    for first in range(0, heads, step):
        names = range(first, min(first + step, heads))
        queries = jnp.concatenate([q_ref[:, h * HD_A : (h + 1) * HD_A] for h in names], axis=0)
        scores = dot_t(queries * BF16(HD_A**-0.5), keys)
        scores = jnp.where(jnp.concatenate([visible] * len(names), axis=0), scores, -jnp.inf)
        peak = jnp.max(scores, axis=-1, keepdims=True)
        weights = jnp.exp(scores - peak)
        total = jnp.sum(weights, axis=-1, keepdims=True)
        mixed = dot(weights.astype(BF16), values)
        for at, h in enumerate(names):
            part = slice(h * HD_A, (h + 1) * HD_A)
            rows = slice(at * length, (at + 1) * length)
            gate = 1.0 + jnp.exp(-gate_ref[:, part].astype(F32))
            held_ref[:, part] = (mixed[rows] / (total[rows] * gate)).astype(BF16)
            copy = pltpu.make_async_copy(held_ref.at[:, part], out_hbm.at[:, part], sems.at[h])
            copy.start()
            copies.append(copy)
    for copy in copies:
        copy.wait()


def call(kernel, out_shape, operands, flops, scalars=1, outside=0, scratch=(), aliases=None, held=pltpu.VMEM):
    moved = sum(o.size * o.dtype.itemsize for o in operands)
    inside = len(operands) - scalars - outside
    operands = [
        pltpu.with_memory_space_constraint(o, pltpu.HBM) if scalars <= i < scalars + outside else o
        for i, o in enumerate(operands)
    ]
    specs = [pl.BlockSpec(memory_space=pltpu.SMEM)] * scalars
    specs += [pl.BlockSpec(memory_space=pltpu.HBM)] * outside
    specs += [pl.BlockSpec(memory_space=pltpu.VMEM)] * inside
    if held is not pltpu.VMEM and aliases:
        specs[-1] = pl.BlockSpec(memory_space=held)
    return pl.pallas_call(
        kernel,
        out_shape=out_shape,
        in_specs=specs,
        out_specs=jax.tree.map(lambda _: pl.BlockSpec(memory_space=held), out_shape),
        scratch_shapes=scratch,
        input_output_aliases=aliases or {},
        compiler_params=pltpu.CompilerParams(vmem_limit_bytes=VMEM_LIMIT),
        cost_estimate=pl.CostEstimate(flops=flops, bytes_accessed=moved, transcendentals=0),
    )(*operands)


def after(value, *others):
    return lax.optimization_barrier((value, *others))[0]


def shards(
    doc_start,
    q_gdn,
    k_gdn,
    v_gdn,
    z_gdn,
    beta_logit,
    log_decay,
    norm_weight,
    q_attn,
    k_attn,
    v_attn,
    gate_attn,
):
    devices = lax.axis_size("seq")
    length = q_gdn.shape[0]
    heads = v_gdn.shape[1] // DV
    local_heads = q_attn.shape[1] // HD_A
    group = QH // KVH
    head_devices = lax.axis_size("head")
    sharers = max(1, min(group // local_heads, head_devices))
    rows = length // sharers
    place = lax.axis_index("seq").astype(jnp.int32)
    head_at = lax.axis_index("head").astype(jnp.int32)
    kv_head = head_at * local_heads // group
    share = head_at % sharers
    scalars = jnp.stack(
        [place * length, kv_head * HD_A] + [(share + sharers - t) % sharers * rows for t in range(sharers)]
    )
    docs = doc_start.reshape(1, length)
    shape = jax.ShapeDtypeStruct
    pieces = PIECES if heads % PIECES == 0 else 1

    sources = (k_gdn, log_decay, beta_logit, docs, v_gdn, norm_weight.reshape(1, DV))
    terms = (
        shape((heads, length, DV), BF16),
        shape((heads, length, DK), BF16),
        shape((heads, DK, DV), F32),
        shape((heads, DK, DK), BF16),
    )
    work = 100 * heads * length * DK * DV
    piece = heads // pieces
    groups = HD_A // DK
    inputs, gain_in = sources[:5], sources[5]
    fresh, *leaving = call(
        opening_kernel,
        (terms[0], *[shape((piece, DK, DV), BF16)] * pieces),
        (scalars, *inputs),
        work,
        outside=len(inputs),
        scratch=[*[pltpu.VMEM(a.shape, a.dtype) for a in inputs], pltpu.SemaphoreType.DMA((len(inputs),))],
    )

    def hand_on(hop, pieces_out):
        return [lax.ppermute(s, "seq", [(hop, hop + 1)]) for s in pieces_out]

    def combined(got, carry, added, between=None):
        done = []
        for at, state in enumerate(got):
            if at == 1 and between:
                state = after(state, *between(done[0]))
            elif done:
                state = after(state, done[-1])
            done.append(
                call(
                    functools.partial(combine_kernel, at * piece),
                    shape((piece, DK, DV), BF16),
                    (state, carry, added),
                    2 * piece * DK * DK * DV,
                    0,
                )
            )
        return done

    def swapped(got, turn):
        pairs = [(i, i // sharers * sharers + (i + turn) % sharers) for i in range(head_devices)]
        return lax.ppermute(got, "head", pairs)

    wanted = min(devices // 2 + 1, devices - 1)
    arrived = [hand_on(0, leaving)]
    fresh, erased, added, carry, unit, gain_in = call(
        second_kernel,
        (*terms, shape((2 * groups * rows, DK), BF16), shape(gain_in.shape, F32)),
        (scalars, *inputs, k_attn, v_attn, gain_in, fresh),
        work,
        aliases={9: 0},
    )
    units = [lax.ppermute(unit, "seq", [(i, i + 1) for i in range(devices - 1)])]
    direct = wanted == devices - 1 and wanted > 1
    farthest = [lax.ppermute(unit, "seq", [(0, wanted)])] if direct else []
    leaving = combined(arrived[-1], carry, added)
    arrived.append(hand_on(1, leaving))
    block = after(units[0], leaving[-1])
    for distance in range(2, wanted + 1 - direct):
        block = lax.ppermute(block, "seq", [(i, i + 1) for i in range(distance - 1, devices - 1)])
        units.append(block)
    units += farthest
    fresh, erased, added, carry = call(
        later_kernel,
        terms,
        (scalars, *inputs, after(fresh, leaving[-1]), erased, added, carry),
        work,
        aliases={6: 0, 7: 1, 8: 2, 9: 3},
    )
    def queries(first):
        mixing.extend(call(
            query_kernel,
            (
                shape((heads, length, DV), F32),
                shape((heads, length, DK), BF16),
                shape((heads, length, DV), F32),
            ),
            (
                *(scalars, inputs[3], inputs[2], inputs[1], q_gdn, inputs[0], z_gdn, gain_in),
                *(after(fresh, first), erased),
            ),
            work,
        ))
        return mixing[:1]

    mixing = []
    queries(fresh)
    for hop in range(2, devices - 1):
        got = [after(arrived[-1][0], mixing[0]), *arrived[-1][1:]] if hop == 2 else arrived[-1]
        leaving = combined(got, carry, added)
        arrived.append(hand_on(hop, leaving))
    local_out, reach, gain = mixing

    layout, sections = [], []
    for distance, got in enumerate(units, 1):
        for turn in range(sharers):
            layout.append((distance, turn))
            sections.append(swapped(after(got, leaving[-1]), turn) if turn else got)
    attn_out = call(
        functools.partial(attention_kernel, (devices // 2 + 1) * length, layout),
        shape(q_attn.shape, BF16),
        (scalars, inputs[3], q_attn, gate_attn, k_attn, v_attn, *sections),
        4 * local_heads * length * length * (wanted + 1) * HD_A,
        scratch=[pltpu.VMEM(q_attn.shape, BF16), pltpu.SemaphoreType.DMA((local_heads,))],
        held=pltpu.HBM,
    )
    ready = []
    for at in range(pieces):
        states = [got[at] for got in arrived]
        operands = (*states, after(local_out, attn_out), reach, gain)
        cost = 2 * piece * length * DK * DV
        if at < pieces - 1:
            ready.append(
                call(
                    functools.partial(piece_kernel, at * piece, len(states)),
                    shape((length, piece * DV), BF16),
                    operands,
                    cost,
                    0,
                )
            )
    gdn_out = call(
        functools.partial(output_kernel, at * piece, len(states)),
        shape(v_gdn.shape, BF16),
        (*operands, *ready),
        cost,
        0,
        scratch=[pltpu.VMEM((length, piece * DV), BF16), pltpu.SemaphoreType.DMA((pieces,))],
        held=pltpu.HBM,
    )
    return (gdn_out, attn_out)


def solution(mesh):
    tokens = P(("groups", "seq"))
    both = P(("groups", "seq"), "head")
    return jax.shard_map(
        shards,
        mesh=mesh,
        in_specs=(
            tokens,
            both,
            both,
            both,
            both,
            P("head", ("groups", "seq")),
            P("head", ("groups", "seq")),
            P(),
            both,
            P(("groups", "seq"), None),
            P(("groups", "seq"), None),
            both,
        ),
        out_specs=(both, both),
        check_vma=False,
    )
```

```python
import functools

import jax
import jax.numpy as jnp
from jax import lax
from jax.experimental import pallas as pl
from jax.experimental.pallas import tpu as pltpu
from jax.sharding import PartitionSpec as P

DK = 128
DV = 128
QH = 16
KVH = 2
HD_A = 256
EPS = 1e-06
VMEM_LIMIT = 48 * 1024 * 1024
PIECES = 2

F32 = jnp.float32
BF16 = jnp.bfloat16


def dot(a, b):
    return jnp.dot(a, b, preferred_element_type=F32)


def dot_t(a, b):
    return lax.dot_general(a, b, (((1,), (1,)), ((), ())), preferred_element_type=F32)


def prefix_sums(rows):
    count, length = rows.shape
    first = rows.astype(BF16)
    rest = rows - first.astype(F32)
    second = rest.astype(BF16)
    third = (rest - second.astype(F32)).astype(BF16)
    t_at = lax.broadcasted_iota(jnp.int32, (length, length), 0)
    i_at = lax.broadcasted_iota(jnp.int32, (length, length), 1)
    ones = (t_at <= i_at).astype(F32).astype(BF16)
    return dot(first, ones) + dot(second, ones) + dot(third, ones)


def columns_of(rows):
    count, length = rows.shape
    padded = jnp.concatenate([rows, jnp.zeros((length - count, length), F32)], axis=0)
    return padded.T


def diagonal_row(square, same_place):
    return jnp.sum(jnp.where(same_place, square, 0.0), axis=0, keepdims=True)


def places(length):
    row = lax.broadcasted_iota(jnp.int32, (length, length), 0)
    col = lax.broadcasted_iota(jnp.int32, (length, length), 1)
    return row, col


def upper_rows(square, size):
    return jnp.concatenate([square[i : i + size] for i in range(size, square.shape[0], 2 * size)], axis=0)


def state_terms(scalar_ref, inputs, u_ref, w_ref=None, a_ref=None, m_ref=None, send_refs=()):
    k_ref, gate_ref, beta_ref, doc_ref, v_ref = inputs
    doc = doc_ref[...]
    anchor = scalar_ref[0]
    length = k_ref.shape[0]
    heads = beta_ref.shape[0]
    key_heads = k_ref.shape[1] // DK
    repeat = heads // key_heads
    row, col = places(length)
    beta = jax.nn.sigmoid(beta_ref[...])
    running = prefix_sums(gate_ref[...])
    keys = [k_ref[:, g * DK : (g + 1) * DK] for g in range(key_heads)]
    grams = [dot_t(k, k) for k in keys]
    squares = [diagonal_row(g, row == col) + EPS for g in grams]
    log_inv = [-0.5 * jnp.log(s) for s in squares]
    inv = [lax.rsqrt(s) for s in squares]
    log_rows = jnp.concatenate([log_inv[h // repeat] for h in range(heads)], axis=0)
    cols = columns_of(
        jnp.concatenate([running + log_rows, jnp.broadcast_to(doc.astype(F32), (8, length))], axis=0)
    )
    doc_col = cols[:, heads : heads + 1]
    place = (anchor + col).astype(F32)
    strict = (doc_col <= place) & (col < row)
    tail_same = doc[:, length - 1 : length] <= (anchor + col[:1, :])
    systems = []
    for h in range(heads):
        spread = cols[:, h : h + 1] - running[h : h + 1, :]
        decay = jnp.where(strict, jnp.exp(spread), 0.0)
        weight = beta[h : h + 1, :] * inv[h // repeat]
        systems.append(decay * grams[h // repeat] * weight)
    differ = row ^ col
    diagonal = differ < 8
    strip_row = lax.broadcasted_iota(jnp.int32, (8, length), 0)
    strip_col = lax.broadcasted_iota(jnp.int32, (8, length), 1)
    lead = strip_col // 8 * 8
    unit = jnp.where(strip_row == strip_col - lead, 1.0, 0.0)
    strips = []
    for n in systems:
        kept = jnp.where(diagonal, n, 0.0)
        parts = [kept[at : at + 8] for at in range(0, length, 8)]
        while len(parts) > 1:
            parts = [x + y for x, y in zip(parts[::2], parts[1::2])]
        strips.append(parts[0])
    solved = [unit] * heads
    for step in range(7):
        picked = [jnp.take_along_axis(n, lead + step, axis=1) for n in strips]
        solved = [x - p * x[step : step + 1] for x, p in zip(solved, picked)]
    inverse = [jnp.where(diagonal, jnp.concatenate([x] * (length // 8), axis=0), 0.0) for x in solved]
    level = 3
    while (1 << level) < length:
        size = 1 << level
        starts = range(size, length, 2 * size)
        mask = (upper_rows(differ, size) >> level) == 1
        kept = [jnp.where(mask, upper_rows(n, size), 0.0).astype(BF16) for n in systems]
        inner = [dot(n, x.astype(BF16)) for n, x in zip(kept, inverse)]
        spare = jnp.zeros((size, length), F32)
        inner = [
            jnp.concatenate([p for i in range(len(starts)) for p in (spare, y[i * size : (i + 1) * size])], axis=0)
            for y in inner
        ]
        outer = [dot(upper_rows(x, size).astype(BF16), y.astype(BF16)) for x, y in zip(inverse, inner)]
        inverse = [
            jnp.concatenate(
                [
                    p
                    for j, i in enumerate(starts)
                    for p in (x[i - size : i], x[i : i + size] - o[j * size : (j + 1) * size])
                ],
                axis=0,
            )
            for x, o in zip(inverse, outer)
        ]
        level += 1
    keys_t = [k.astype(F32).T for k in keys]
    for h in range(heads):
        g = h // repeat
        run = running[h : h + 1, :]
        u = dot(inverse[h].astype(BF16), v_ref[:, h * DV : (h + 1) * DV]).astype(BF16)
        u_ref[h] = u
        tail = jnp.exp(run[:, length - 1 : length] - run)
        tail = jnp.where(tail_same, tail, 0.0) * beta[h : h + 1, :] * inv[g]
        tail_keys = (keys_t[g] * tail).astype(BF16)
        a = dot(tail_keys, u)
        if send_refs:
            piece = heads // len(send_refs)
            send_refs[h // piece][h % piece] = a.astype(BF16)
            continue
        a_ref[h] = a
        entry = jnp.where(doc < anchor, jnp.exp(run), 0.0)
        w = dot((inverse[h] * (entry * inv[g])).astype(BF16), keys[g]).astype(BF16)
        w_ref[h] = w
        m_ref[h] = (jnp.where(row == col, entry[:, length - 1 : length], 0.0) - dot(tail_keys, w)).astype(BF16)


def opening_kernel(scalar_ref, *refs):
    sources, u_ref, send_refs = refs[:5], refs[5], refs[6:-6]
    inputs, sems = refs[-6:-1], refs[-1]

    @pl.when(scalar_ref[0] == 0)
    def _():
        copies = [pltpu.make_async_copy(a, b, sems.at[i]) for i, (a, b) in enumerate(zip(sources, inputs))]
        for copy in copies:
            copy.start()
        for copy in copies:
            copy.wait()
        state_terms(scalar_ref, inputs, u_ref, send_refs=send_refs)


def second_kernel(scalar_ref, *refs):
    inputs, (ka_ref, va_ref, gain_ref, _) = refs[:5], refs[5:9]
    u_ref, w_ref, a_ref, m_ref, unit_ref, kept_ref = refs[9:]
    kept_ref[...] = gain_ref[...]
    length = u_ref.shape[1]
    groups = HD_A // DK
    rows = unit_ref.shape[0] // (2 * groups)
    begin = pl.multiple_of(scalar_ref[2], rows)
    for at in range(2 * groups):
        lanes = pl.ds(pl.multiple_of(scalar_ref[1] + at % groups * DK, DK), DK)
        unit_ref[at * rows : (at + 1) * rows] = (ka_ref, va_ref)[at // groups][pl.ds(begin, rows), lanes]

    @pl.when(scalar_ref[0] == 0)
    def _():
        w_ref[...] = jnp.zeros(w_ref.shape, BF16)

    @pl.when(scalar_ref[0] == length)
    def _():
        state_terms(scalar_ref, inputs, u_ref, w_ref, a_ref, m_ref)


def later_kernel(scalar_ref, *refs):
    inputs, outs = refs[:5], refs[9:]
    length = outs[0].shape[1]

    @pl.when(scalar_ref[0] > length)
    def _():
        state_terms(scalar_ref, inputs, *outs)


def query_kernel(
    scalar_ref, doc_ref, beta_ref, gate_ref, q_ref, k_ref, z_ref, gain_ref, u_ref, w_ref, local_ref, reach_ref, gz_ref
):
    length = k_ref.shape[0]
    heads = beta_ref.shape[0]
    key_heads = k_ref.shape[1] // DK
    repeat = heads // key_heads
    anchor = scalar_ref[0]
    row, col = places(length)
    beta = jax.nn.sigmoid(beta_ref[...])
    running = prefix_sums(gate_ref[...])
    doc = doc_ref[...]
    keys = [k_ref[:, g * DK : (g + 1) * DK] for g in range(key_heads)]
    queries = [q_ref[:, g * DK : (g + 1) * DK] for g in range(key_heads)]
    inv = [lax.rsqrt(diagonal_row(dot_t(k, k), row == col) + EPS) for k in keys]
    log_q = [-0.5 * jnp.log(diagonal_row(dot_t(q, q), row == col) + EPS) for q in queries]
    log_rows = jnp.concatenate([log_q[h // repeat] for h in range(heads)], axis=0)
    cols = columns_of(
        jnp.concatenate([running + log_rows, jnp.broadcast_to(doc.astype(F32), (8, length))], axis=0)
    )
    doc_col = cols[:, heads : heads + 1]
    place = (anchor + col).astype(F32)
    same = (doc_col <= place) & (col <= row)
    alive_col = doc_col < anchor.astype(F32)
    cross = [dot_t(q, k) for q, k in zip(queries, keys)]
    for h in range(heads):
        g = h // repeat
        weight = beta[h : h + 1, :] * inv[g]
        decay = jnp.where(same, jnp.exp(cols[:, h : h + 1] - running[h : h + 1, :]), 0.0)
        scores = (decay * cross[g] * weight).astype(BF16)
        local_ref[h] = dot(scores, u_ref[h])
        lead = jnp.where(alive_col, jnp.exp(cols[:, h : h + 1]), 0.0)
        reach_ref[h] = (lead * queries[g].astype(F32) - dot(scores, w_ref[h])).astype(BF16)
    z = z_ref[...].astype(F32)
    gate = z / (1.0 + jnp.exp(-z))
    for h in range(heads):
        gz_ref[h] = gate[:, h * DV : (h + 1) * DV] * gain_ref[...]


def combine_kernel(begin, s_ref, m_ref, a_ref, out_ref):
    for h in range(s_ref.shape[0]):
        out_ref[h] = (dot(m_ref[begin + h], s_ref[h]) + a_ref[begin + h]).astype(BF16)


def normed_piece(begin, states, local_ref, reach_ref, gz_ref, out_ref, columns):
    for at in range(states[0].shape[0]):
        state = states[0][at]
        for other in states[1:]:
            state = state + other[at]
        h = begin + at
        mixed = local_ref[h] + dot(reach_ref[h], state)
        factor = lax.rsqrt(jnp.mean(mixed * mixed, axis=-1, keepdims=True) + EPS)
        spot = columns + at * DV
        out_ref[:, spot : spot + DV] = (mixed * factor * gz_ref[h]).astype(BF16)


def piece_kernel(begin, hops, *refs):
    normed_piece(begin, refs[:hops], *refs[hops:], 0)


def output_kernel(begin, hops, *refs):
    states, terms, ready = refs[:hops], refs[hops : hops + 3], refs[hops + 3 : -3]
    out_hbm, held_ref, sems = refs[-3:]
    copies = []
    spot = 0
    for at, part in enumerate((*ready, held_ref)):
        if part is held_ref:
            normed_piece(begin, states, *terms, held_ref, 0)
        width = part.shape[1]
        copies.append(pltpu.make_async_copy(part, out_hbm.at[:, spot : spot + width], sems.at[at]))
        copies[-1].start()
        spot += width
    for copy in copies:
        copy.wait()


def attention_kernel(window, layout, scalar_ref, doc_ref, q_ref, gate_ref, k_ref, v_ref, *refs):
    units, (out_hbm, held_ref, sems) = refs[:-3], refs[-3:]
    length = q_ref.shape[0]
    heads = q_ref.shape[1] // HD_A
    groups = HD_A // DK
    anchor = scalar_ref[0]
    docs = columns_of(jnp.broadcast_to(doc_ref[...].astype(F32), (8, length)))[:, :1].astype(jnp.int32)
    q_place = anchor + lax.broadcasted_iota(jnp.int32, (length, 1), 0)
    lower = jnp.maximum(jnp.maximum(docs, q_place - window + 1), 0)
    spots = [anchor + lax.broadcasted_iota(jnp.int32, (length, length), 1)]
    wanted = pl.ds(pl.multiple_of(scalar_ref[1], HD_A), HD_A)
    keys, values = [k_ref[:, wanted]], [v_ref[:, wanted]]
    for (distance, turn), unit in zip(layout, units):
        rows = unit.shape[0] // (2 * groups)
        start = anchor - distance * length + scalar_ref[2 + turn]
        spots.append(start + lax.broadcasted_iota(jnp.int32, (length, rows), 1))
        blocks = [unit[at * rows : (at + 1) * rows] for at in range(2 * groups)]
        keys.append(jnp.concatenate(blocks[:groups], axis=1))
        values.append(jnp.concatenate(blocks[groups:], axis=1))
    k_place = jnp.concatenate(spots, axis=1)
    visible = (k_place >= lower) & (k_place <= q_place)
    keys = jnp.concatenate(keys, axis=0)
    values = jnp.concatenate(values, axis=0)
    step = 2
    copies = []
    for first in range(0, heads, step):
        names = range(first, min(first + step, heads))
        queries = jnp.concatenate([q_ref[:, h * HD_A : (h + 1) * HD_A] for h in names], axis=0)
        scores = dot_t(queries * BF16(HD_A**-0.5), keys)
        scores = jnp.where(jnp.concatenate([visible] * len(names), axis=0), scores, -jnp.inf)
        peak = jnp.max(scores, axis=-1, keepdims=True)
        weights = jnp.exp(scores - peak)
        total = jnp.sum(weights, axis=-1, keepdims=True)
        mixed = dot(weights.astype(BF16), values)
        for at, h in enumerate(names):
            part = slice(h * HD_A, (h + 1) * HD_A)
            rows = slice(at * length, (at + 1) * length)
            gate = 1.0 + jnp.exp(-gate_ref[:, part].astype(F32))
            held_ref[:, part] = (mixed[rows] / (total[rows] * gate)).astype(BF16)
            copy = pltpu.make_async_copy(held_ref.at[:, part], out_hbm.at[:, part], sems.at[h])
            copy.start()
            copies.append(copy)
    for copy in copies:
        copy.wait()


def call(kernel, out_shape, operands, flops, scalars=1, outside=0, scratch=(), aliases=None, held=pltpu.VMEM):
    moved = sum(o.size * o.dtype.itemsize for o in operands)
    inside = len(operands) - scalars - outside
    operands = [
        pltpu.with_memory_space_constraint(o, pltpu.HBM) if scalars <= i < scalars + outside else o
        for i, o in enumerate(operands)
    ]
    specs = [pl.BlockSpec(memory_space=pltpu.SMEM)] * scalars
    specs += [pl.BlockSpec(memory_space=pltpu.HBM)] * outside
    specs += [pl.BlockSpec(memory_space=pltpu.VMEM)] * inside
    if held is not pltpu.VMEM and aliases:
        specs[-1] = pl.BlockSpec(memory_space=held)
    return pl.pallas_call(
        kernel,
        out_shape=out_shape,
        in_specs=specs,
        out_specs=jax.tree.map(lambda _: pl.BlockSpec(memory_space=held), out_shape),
        scratch_shapes=scratch,
        input_output_aliases=aliases or {},
        compiler_params=pltpu.CompilerParams(vmem_limit_bytes=VMEM_LIMIT),
        cost_estimate=pl.CostEstimate(flops=flops, bytes_accessed=moved, transcendentals=0),
    )(*operands)


def after(value, *others):
    return lax.optimization_barrier((value, *others))[0]


def shards(
    doc_start,
    q_gdn,
    k_gdn,
    v_gdn,
    z_gdn,
    beta_logit,
    log_decay,
    norm_weight,
    q_attn,
    k_attn,
    v_attn,
    gate_attn,
):
    devices = lax.axis_size("seq")
    length = q_gdn.shape[0]
    heads = v_gdn.shape[1] // DV
    local_heads = q_attn.shape[1] // HD_A
    group = QH // KVH
    head_devices = lax.axis_size("head")
    sharers = max(1, min(group // local_heads, head_devices))
    rows = length // sharers
    place = lax.axis_index("seq").astype(jnp.int32)
    head_at = lax.axis_index("head").astype(jnp.int32)
    kv_head = head_at * local_heads // group
    share = head_at % sharers
    scalars = jnp.stack(
        [place * length, kv_head * HD_A] + [(share + sharers - t) % sharers * rows for t in range(sharers)]
    )
    docs = doc_start.reshape(1, length)
    shape = jax.ShapeDtypeStruct
    pieces = PIECES if heads % PIECES == 0 else 1

    sources = (k_gdn, log_decay, beta_logit, docs, v_gdn, norm_weight.reshape(1, DV))
    terms = (
        shape((heads, length, DV), BF16),
        shape((heads, length, DK), BF16),
        shape((heads, DK, DV), F32),
        shape((heads, DK, DK), BF16),
    )
    work = 100 * heads * length * DK * DV
    piece = heads // pieces
    groups = HD_A // DK
    inputs, gain_in = sources[:5], sources[5]
    fresh, *leaving = call(
        opening_kernel,
        (terms[0], *[shape((piece, DK, DV), BF16)] * pieces),
        (scalars, *inputs),
        work,
        outside=len(inputs),
        scratch=[*[pltpu.VMEM(a.shape, a.dtype) for a in inputs], pltpu.SemaphoreType.DMA((len(inputs),))],
    )

    def hand_on(hop, pieces_out):
        return [lax.ppermute(s, "seq", [(hop, hop + 1)]) for s in pieces_out]

    def combined(got, carry, added, between=None):
        done = []
        for at, state in enumerate(got):
            if at == 1 and between:
                state = after(state, *between(done[0]))
            elif done:
                state = after(state, done[-1])
            done.append(
                call(
                    functools.partial(combine_kernel, at * piece),
                    shape((piece, DK, DV), BF16),
                    (state, carry, added),
                    2 * piece * DK * DK * DV,
                    0,
                )
            )
        return done

    def swapped(got, turn):
        pairs = [(i, i // sharers * sharers + (i + turn) % sharers) for i in range(head_devices)]
        return lax.ppermute(got, "head", pairs)

    wanted = min(devices // 2 + 1, devices - 1)
    arrived = [hand_on(0, leaving)]
    fresh, erased, added, carry, unit, gain_in = call(
        second_kernel,
        (*terms, shape((2 * groups * rows, DK), BF16), shape(gain_in.shape, F32)),
        (scalars, *inputs, k_attn, v_attn, gain_in, fresh),
        work,
        aliases={9: 0},
    )
    units = [lax.ppermute(unit, "seq", [(i, i + 1) for i in range(devices - 1)])]
    direct = wanted == devices - 1 and wanted > 1
    farthest = [lax.ppermute(unit, "seq", [(0, wanted)])] if direct else []
    leaving = combined(arrived[-1], carry, added)
    arrived.append(hand_on(1, leaving))
    block = after(units[0], leaving[-1])
    for distance in range(2, wanted + 1 - direct):
        block = lax.ppermute(block, "seq", [(i, i + 1) for i in range(distance - 1, devices - 1)])
        units.append(block)
    units += farthest
    fresh, erased, added, carry = call(
        later_kernel,
        terms,
        (scalars, *inputs, after(fresh, leaving[-1]), erased, added, carry),
        work,
        aliases={6: 0, 7: 1, 8: 2, 9: 3},
    )
    def queries(first):
        mixing.extend(call(
            query_kernel,
            (
                shape((heads, length, DV), F32),
                shape((heads, length, DK), BF16),
                shape((heads, length, DV), F32),
            ),
            (
                *(scalars, inputs[3], inputs[2], inputs[1], q_gdn, inputs[0], z_gdn, gain_in),
                *(after(fresh, first), erased),
            ),
            3 * work,
        ))
        return mixing[:1]

    mixing = []
    queries(fresh)
    for hop in range(2, devices - 1):
        got = [after(arrived[-1][0], mixing[0]), *arrived[-1][1:]] if hop == 2 else arrived[-1]
        leaving = combined(got, carry, added)
        arrived.append(hand_on(hop, leaving))
    local_out, reach, gain = mixing

    layout, sections = [], []
    for distance, got in enumerate(units, 1):
        for turn in range(sharers):
            layout.append((distance, turn))
            sections.append(swapped(after(got, leaving[-1]), turn) if turn else got)
    attn_out = call(
        functools.partial(attention_kernel, (devices // 2 + 1) * length, layout),
        shape(q_attn.shape, BF16),
        (scalars, inputs[3], q_attn, gate_attn, k_attn, v_attn, *sections),
        4 * local_heads * length * length * (wanted + 1) * HD_A,
        scratch=[pltpu.VMEM(q_attn.shape, BF16), pltpu.SemaphoreType.DMA((local_heads,))],
        held=pltpu.HBM,
    )
    ready = []
    for at in range(pieces):
        states = [got[at] for got in arrived]
        operands = (*states, after(local_out, attn_out), reach, gain)
        cost = 2 * piece * length * DK * DV
        if at < pieces - 1:
            ready.append(
                call(
                    functools.partial(piece_kernel, at * piece, len(states)),
                    shape((length, piece * DV), BF16),
                    operands,
                    cost,
                    0,
                )
            )
    gdn_out = call(
        functools.partial(output_kernel, at * piece, len(states)),
        shape(v_gdn.shape, BF16),
        (*operands, *ready),
        cost,
        0,
        scratch=[pltpu.VMEM((length, piece * DV), BF16), pltpu.SemaphoreType.DMA((pieces,))],
        held=pltpu.HBM,
    )
    return (gdn_out, attn_out)


def solution(mesh):
    tokens = P(("groups", "seq"))
    both = P(("groups", "seq"), "head")
    return jax.shard_map(
        shards,
        mesh=mesh,
        in_specs=(
            tokens,
            both,
            both,
            both,
            both,
            P("head", ("groups", "seq")),
            P("head", ("groups", "seq")),
            P(),
            both,
            P(("groups", "seq"), None),
            P(("groups", "seq"), None),
            both,
        ),
        out_specs=(both, both),
        check_vma=False,
    )
```

```python
import functools

import jax
import jax.numpy as jnp
from jax import lax
from jax.experimental import pallas as pl
from jax.experimental.pallas import tpu as pltpu
from jax.sharding import PartitionSpec as P

DK = 128
DV = 128
QH = 16
KVH = 2
HD_A = 256
EPS = 1e-06
VMEM_LIMIT = 48 * 1024 * 1024
PIECES = 2

F32 = jnp.float32
BF16 = jnp.bfloat16


def dot(a, b):
    return jnp.dot(a, b, preferred_element_type=F32)


def dot_t(a, b):
    return lax.dot_general(a, b, (((1,), (1,)), ((), ())), preferred_element_type=F32)


def prefix_sums(rows):
    count, length = rows.shape
    first = rows.astype(BF16)
    rest = rows - first.astype(F32)
    second = rest.astype(BF16)
    third = (rest - second.astype(F32)).astype(BF16)
    t_at = lax.broadcasted_iota(jnp.int32, (length, length), 0)
    i_at = lax.broadcasted_iota(jnp.int32, (length, length), 1)
    ones = (t_at <= i_at).astype(F32).astype(BF16)
    return dot(first, ones) + dot(second, ones) + dot(third, ones)


def columns_of(rows):
    count, length = rows.shape
    padded = jnp.concatenate([rows, jnp.zeros((length - count, length), F32)], axis=0)
    return padded.T


def diagonal_row(square, same_place):
    return jnp.sum(jnp.where(same_place, square, 0.0), axis=0, keepdims=True)


def places(length):
    row = lax.broadcasted_iota(jnp.int32, (length, length), 0)
    col = lax.broadcasted_iota(jnp.int32, (length, length), 1)
    return row, col


def upper_rows(square, size):
    return jnp.concatenate([square[i : i + size] for i in range(size, square.shape[0], 2 * size)], axis=0)


def state_terms(scalar_ref, inputs, u_ref, w_ref=None, a_ref=None, m_ref=None, send_refs=()):
    k_ref, gate_ref, beta_ref, doc_ref, v_ref = inputs
    doc = doc_ref[...]
    anchor = scalar_ref[0]
    length = k_ref.shape[0]
    heads = beta_ref.shape[0]
    key_heads = k_ref.shape[1] // DK
    repeat = heads // key_heads
    row, col = places(length)
    beta = jax.nn.sigmoid(beta_ref[...])
    running = prefix_sums(gate_ref[...])
    keys = [k_ref[:, g * DK : (g + 1) * DK] for g in range(key_heads)]
    grams = [dot_t(k, k) for k in keys]
    squares = [diagonal_row(g, row == col) + EPS for g in grams]
    log_inv = [-0.5 * jnp.log(s) for s in squares]
    inv = [lax.rsqrt(s) for s in squares]
    log_rows = jnp.concatenate([log_inv[h // repeat] for h in range(heads)], axis=0)
    cols = columns_of(
        jnp.concatenate([running + log_rows, jnp.broadcast_to(doc.astype(F32), (8, length))], axis=0)
    )
    doc_col = cols[:, heads : heads + 1]
    place = (anchor + col).astype(F32)
    strict = (doc_col <= place) & (col < row)
    tail_same = doc[:, length - 1 : length] <= (anchor + col[:1, :])
    systems = []
    for h in range(heads):
        spread = cols[:, h : h + 1] - running[h : h + 1, :]
        decay = jnp.where(strict, jnp.exp(spread), 0.0)
        weight = beta[h : h + 1, :] * inv[h // repeat]
        systems.append(decay * grams[h // repeat] * weight)
    differ = row ^ col
    diagonal = differ < 8
    strip_row = lax.broadcasted_iota(jnp.int32, (8, length), 0)
    strip_col = lax.broadcasted_iota(jnp.int32, (8, length), 1)
    lead = strip_col // 8 * 8
    unit = jnp.where(strip_row == strip_col - lead, 1.0, 0.0)
    strips = []
    for n in systems:
        kept = jnp.where(diagonal, n, 0.0)
        parts = [kept[at : at + 8] for at in range(0, length, 8)]
        while len(parts) > 1:
            parts = [x + y for x, y in zip(parts[::2], parts[1::2])]
        strips.append(parts[0])
    solved = [unit] * heads
    for step in range(7):
        picked = [jnp.take_along_axis(n, lead + step, axis=1) for n in strips]
        solved = [x - p * x[step : step + 1] for x, p in zip(solved, picked)]
    inverse = [jnp.where(diagonal, jnp.concatenate([x] * (length // 8), axis=0), 0.0) for x in solved]
    level = 3
    while (1 << level) < length:
        size = 1 << level
        starts = range(size, length, 2 * size)
        mask = (upper_rows(differ, size) >> level) == 1
        kept = [jnp.where(mask, upper_rows(n, size), 0.0).astype(BF16) for n in systems]
        inner = [dot(n, x.astype(BF16)) for n, x in zip(kept, inverse)]
        spare = jnp.zeros((size, length), F32)
        inner = [
            jnp.concatenate([p for i in range(len(starts)) for p in (spare, y[i * size : (i + 1) * size])], axis=0)
            for y in inner
        ]
        outer = [dot(upper_rows(x, size).astype(BF16), y.astype(BF16)) for x, y in zip(inverse, inner)]
        inverse = [
            jnp.concatenate(
                [
                    p
                    for j, i in enumerate(starts)
                    for p in (x[i - size : i], x[i : i + size] - o[j * size : (j + 1) * size])
                ],
                axis=0,
            )
            for x, o in zip(inverse, outer)
        ]
        level += 1
    keys_t = [k.astype(F32).T for k in keys]
    for h in range(heads):
        g = h // repeat
        run = running[h : h + 1, :]
        u = dot(inverse[h].astype(BF16), v_ref[:, h * DV : (h + 1) * DV]).astype(BF16)
        u_ref[h] = u
        tail = jnp.exp(run[:, length - 1 : length] - run)
        tail = jnp.where(tail_same, tail, 0.0) * beta[h : h + 1, :] * inv[g]
        tail_keys = (keys_t[g] * tail).astype(BF16)
        a = dot(tail_keys, u)
        if send_refs:
            piece = heads // len(send_refs)
            send_refs[h // piece][h % piece] = a.astype(BF16)
            continue
        a_ref[h] = a
        entry = jnp.where(doc < anchor, jnp.exp(run), 0.0)
        w = dot((inverse[h] * (entry * inv[g])).astype(BF16), keys[g]).astype(BF16)
        w_ref[h] = w
        m_ref[h] = (jnp.where(row == col, entry[:, length - 1 : length], 0.0) - dot(tail_keys, w)).astype(BF16)


def opening_kernel(scalar_ref, *refs):
    sources, u_ref, send_refs = refs[:5], refs[5], refs[6:-6]
    inputs, sems = refs[-6:-1], refs[-1]

    @pl.when(scalar_ref[0] == 0)
    def _():
        copies = [pltpu.make_async_copy(a, b, sems.at[i]) for i, (a, b) in enumerate(zip(sources, inputs))]
        for copy in copies:
            copy.start()
        for copy in copies:
            copy.wait()
        state_terms(scalar_ref, inputs, u_ref, send_refs=send_refs)


def second_kernel(scalar_ref, *refs):
    inputs, (ka_ref, va_ref, gain_ref, _) = refs[:5], refs[5:9]
    u_ref, w_ref, a_ref, m_ref, unit_ref, kept_ref = refs[9:]
    kept_ref[...] = gain_ref[...]
    length = u_ref.shape[1]
    groups = HD_A // DK
    rows = unit_ref.shape[0] // (2 * groups)
    begin = pl.multiple_of(scalar_ref[2], rows)
    for at in range(2 * groups):
        lanes = pl.ds(pl.multiple_of(scalar_ref[1] + at % groups * DK, DK), DK)
        unit_ref[at * rows : (at + 1) * rows] = (ka_ref, va_ref)[at // groups][pl.ds(begin, rows), lanes]

    @pl.when(scalar_ref[0] == 0)
    def _():
        w_ref[...] = jnp.zeros(w_ref.shape, BF16)

    @pl.when(scalar_ref[0] == length)
    def _():
        state_terms(scalar_ref, inputs, u_ref, w_ref, a_ref, m_ref)


def later_kernel(scalar_ref, *refs):
    inputs, outs = refs[:5], refs[9:]
    length = outs[0].shape[1]

    @pl.when(scalar_ref[0] > length)
    def _():
        state_terms(scalar_ref, inputs, *outs)


def query_kernel(
    scalar_ref, doc_ref, beta_ref, gate_ref, q_ref, k_ref, z_ref, gain_ref, u_ref, w_ref, local_ref, reach_ref, gz_ref
):
    length = k_ref.shape[0]
    heads = beta_ref.shape[0]
    key_heads = k_ref.shape[1] // DK
    repeat = heads // key_heads
    anchor = scalar_ref[0]
    row, col = places(length)
    beta = jax.nn.sigmoid(beta_ref[...])
    running = prefix_sums(gate_ref[...])
    doc = doc_ref[...]
    keys = [k_ref[:, g * DK : (g + 1) * DK] for g in range(key_heads)]
    queries = [q_ref[:, g * DK : (g + 1) * DK] for g in range(key_heads)]
    inv = [lax.rsqrt(diagonal_row(dot_t(k, k), row == col) + EPS) for k in keys]
    log_q = [-0.5 * jnp.log(diagonal_row(dot_t(q, q), row == col) + EPS) for q in queries]
    log_rows = jnp.concatenate([log_q[h // repeat] for h in range(heads)], axis=0)
    cols = columns_of(
        jnp.concatenate([running + log_rows, jnp.broadcast_to(doc.astype(F32), (8, length))], axis=0)
    )
    doc_col = cols[:, heads : heads + 1]
    place = (anchor + col).astype(F32)
    same = (doc_col <= place) & (col <= row)
    alive_col = doc_col < anchor.astype(F32)
    cross = [dot_t(q, k) for q, k in zip(queries, keys)]
    for h in range(heads):
        g = h // repeat
        weight = beta[h : h + 1, :] * inv[g]
        decay = jnp.where(same, jnp.exp(cols[:, h : h + 1] - running[h : h + 1, :]), 0.0)
        scores = (decay * cross[g] * weight).astype(BF16)
        local_ref[h] = dot(scores, u_ref[h])
        lead = jnp.where(alive_col, jnp.exp(cols[:, h : h + 1]), 0.0)
        reach_ref[h] = (lead * queries[g].astype(F32) - dot(scores, w_ref[h])).astype(BF16)
    z = z_ref[...].astype(F32)
    gate = z / (1.0 + jnp.exp(-z))
    for h in range(heads):
        gz_ref[h] = gate[:, h * DV : (h + 1) * DV] * gain_ref[...]


def combine_kernel(begin, s_ref, m_ref, a_ref, out_ref):
    for h in range(s_ref.shape[0]):
        out_ref[h] = (dot(m_ref[begin + h], s_ref[h]) + a_ref[begin + h]).astype(BF16)


def normed_piece(begin, states, local_ref, reach_ref, gz_ref, out_ref, columns):
    for at in range(states[0].shape[0]):
        state = states[0][at]
        for other in states[1:]:
            state = state + other[at]
        h = begin + at
        mixed = local_ref[h] + dot(reach_ref[h], state)
        factor = lax.rsqrt(jnp.mean(mixed * mixed, axis=-1, keepdims=True) + EPS)
        spot = columns + at * DV
        out_ref[:, spot : spot + DV] = (mixed * factor * gz_ref[h]).astype(BF16)


def piece_kernel(begin, hops, *refs):
    normed_piece(begin, refs[:hops], *refs[hops:], 0)


def output_kernel(begin, hops, *refs):
    states, terms, attn_ref, ready = refs[:hops], refs[hops : hops + 3], refs[hops + 3], refs[hops + 4 : -4]
    out_hbm, attn_hbm, held_ref, sems = refs[-4:]
    copies = [pltpu.make_async_copy(attn_ref, attn_hbm, sems.at[len(ready) + 1])]
    copies[0].start()
    spot = 0
    for at, part in enumerate((*ready, held_ref)):
        if part is held_ref:
            normed_piece(begin, states, *terms, held_ref, 0)
        width = part.shape[1]
        copies.append(pltpu.make_async_copy(part, out_hbm.at[:, spot : spot + width], sems.at[at]))
        copies[-1].start()
        spot += width
    for copy in copies:
        copy.wait()


def attention_kernel(window, layout, scalar_ref, doc_ref, q_ref, gate_ref, k_ref, v_ref, *refs):
    units, out_ref = refs[:-1], refs[-1]
    length = q_ref.shape[0]
    heads = q_ref.shape[1] // HD_A
    groups = HD_A // DK
    anchor = scalar_ref[0]
    docs = columns_of(jnp.broadcast_to(doc_ref[...].astype(F32), (8, length)))[:, :1].astype(jnp.int32)
    q_place = anchor + lax.broadcasted_iota(jnp.int32, (length, 1), 0)
    lower = jnp.maximum(jnp.maximum(docs, q_place - window + 1), 0)
    spots = [anchor + lax.broadcasted_iota(jnp.int32, (length, length), 1)]
    wanted = pl.ds(pl.multiple_of(scalar_ref[1], HD_A), HD_A)
    keys, values = [k_ref[:, wanted]], [v_ref[:, wanted]]
    for (distance, turn), unit in zip(layout, units):
        rows = unit.shape[0] // (2 * groups)
        start = anchor - distance * length + scalar_ref[2 + turn]
        spots.append(start + lax.broadcasted_iota(jnp.int32, (length, rows), 1))
        blocks = [unit[at * rows : (at + 1) * rows] for at in range(2 * groups)]
        keys.append(jnp.concatenate(blocks[:groups], axis=1))
        values.append(jnp.concatenate(blocks[groups:], axis=1))
    k_place = jnp.concatenate(spots, axis=1)
    visible = (k_place >= lower) & (k_place <= q_place)
    keys = jnp.concatenate(keys, axis=0)
    values = jnp.concatenate(values, axis=0)
    step = 2
    for first in range(0, heads, step):
        names = range(first, min(first + step, heads))
        queries = jnp.concatenate([q_ref[:, h * HD_A : (h + 1) * HD_A] for h in names], axis=0)
        scores = dot_t(queries * BF16(HD_A**-0.5), keys)
        scores = jnp.where(jnp.concatenate([visible] * len(names), axis=0), scores, -jnp.inf)
        peak = jnp.max(scores, axis=-1, keepdims=True)
        weights = jnp.exp(scores - peak)
        total = jnp.sum(weights, axis=-1, keepdims=True)
        mixed = dot(weights.astype(BF16), values)
        for at, h in enumerate(names):
            part = slice(h * HD_A, (h + 1) * HD_A)
            rows = slice(at * length, (at + 1) * length)
            gate = 1.0 + jnp.exp(-gate_ref[:, part].astype(F32))
            out_ref[:, part] = (mixed[rows] / (total[rows] * gate)).astype(BF16)


def call(kernel, out_shape, operands, flops, scalars=1, outside=0, scratch=(), aliases=None, held=pltpu.VMEM):
    moved = sum(o.size * o.dtype.itemsize for o in operands)
    inside = len(operands) - scalars - outside
    operands = [
        pltpu.with_memory_space_constraint(o, pltpu.HBM) if scalars <= i < scalars + outside else o
        for i, o in enumerate(operands)
    ]
    specs = [pl.BlockSpec(memory_space=pltpu.SMEM)] * scalars
    specs += [pl.BlockSpec(memory_space=pltpu.HBM)] * outside
    specs += [pl.BlockSpec(memory_space=pltpu.VMEM)] * inside
    if held is not pltpu.VMEM and aliases:
        specs[-1] = pl.BlockSpec(memory_space=held)
    return pl.pallas_call(
        kernel,
        out_shape=out_shape,
        in_specs=specs,
        out_specs=jax.tree.map(lambda _: pl.BlockSpec(memory_space=held), out_shape),
        scratch_shapes=scratch,
        input_output_aliases=aliases or {},
        compiler_params=pltpu.CompilerParams(vmem_limit_bytes=VMEM_LIMIT),
        cost_estimate=pl.CostEstimate(flops=flops, bytes_accessed=moved, transcendentals=0),
    )(*operands)


def after(value, *others):
    return lax.optimization_barrier((value, *others))[0]


def shards(
    doc_start,
    q_gdn,
    k_gdn,
    v_gdn,
    z_gdn,
    beta_logit,
    log_decay,
    norm_weight,
    q_attn,
    k_attn,
    v_attn,
    gate_attn,
):
    devices = lax.axis_size("seq")
    length = q_gdn.shape[0]
    heads = v_gdn.shape[1] // DV
    local_heads = q_attn.shape[1] // HD_A
    group = QH // KVH
    head_devices = lax.axis_size("head")
    sharers = max(1, min(group // local_heads, head_devices))
    rows = length // sharers
    place = lax.axis_index("seq").astype(jnp.int32)
    head_at = lax.axis_index("head").astype(jnp.int32)
    kv_head = head_at * local_heads // group
    share = head_at % sharers
    scalars = jnp.stack(
        [place * length, kv_head * HD_A] + [(share + sharers - t) % sharers * rows for t in range(sharers)]
    )
    docs = doc_start.reshape(1, length)
    shape = jax.ShapeDtypeStruct
    pieces = PIECES if heads % PIECES == 0 else 1

    sources = (k_gdn, log_decay, beta_logit, docs, v_gdn, norm_weight.reshape(1, DV))
    terms = (
        shape((heads, length, DV), BF16),
        shape((heads, length, DK), BF16),
        shape((heads, DK, DV), F32),
        shape((heads, DK, DK), BF16),
    )
    work = 100 * heads * length * DK * DV
    piece = heads // pieces
    groups = HD_A // DK
    inputs, gain_in = sources[:5], sources[5]
    fresh, *leaving = call(
        opening_kernel,
        (terms[0], *[shape((piece, DK, DV), BF16)] * pieces),
        (scalars, *inputs),
        work,
        outside=len(inputs),
        scratch=[*[pltpu.VMEM(a.shape, a.dtype) for a in inputs], pltpu.SemaphoreType.DMA((len(inputs),))],
    )

    def hand_on(hop, pieces_out):
        return [lax.ppermute(s, "seq", [(hop, hop + 1)]) for s in pieces_out]

    def combined(got, carry, added, between=None):
        done = []
        for at, state in enumerate(got):
            if at == 1 and between:
                state = after(state, *between(done[0]))
            elif done:
                state = after(state, done[-1])
            done.append(
                call(
                    functools.partial(combine_kernel, at * piece),
                    shape((piece, DK, DV), BF16),
                    (state, carry, added),
                    2 * piece * DK * DK * DV,
                    0,
                )
            )
        return done

    def swapped(got, turn):
        pairs = [(i, i // sharers * sharers + (i + turn) % sharers) for i in range(head_devices)]
        return lax.ppermute(got, "head", pairs)

    wanted = min(devices // 2 + 1, devices - 1)
    arrived = [hand_on(0, leaving)]
    fresh, erased, added, carry, unit, gain_in = call(
        second_kernel,
        (*terms, shape((2 * groups * rows, DK), BF16), shape(gain_in.shape, F32)),
        (scalars, *inputs, k_attn, v_attn, gain_in, fresh),
        work,
        aliases={9: 0},
    )
    units = [lax.ppermute(unit, "seq", [(i, i + 1) for i in range(devices - 1)])]
    direct = wanted == devices - 1 and wanted > 1
    leaving = combined(arrived[-1], carry, added)
    arrived.append(hand_on(1, leaving))
    farthest = [lax.ppermute(after(unit, leaving[-1]), "seq", [(0, wanted)])] if direct else []
    fresh, erased, added, carry = call(
        later_kernel,
        terms,
        (scalars, *inputs, after(fresh, leaving[-1]), erased, added, carry),
        work,
        aliases={6: 0, 7: 1, 8: 2, 9: 3},
    )
    block = after(units[0], fresh)
    for distance in range(2, wanted + 1 - direct):
        block = lax.ppermute(block, "seq", [(i, i + 1) for i in range(distance - 1, devices - 1)])
        units.append(block)
    units += farthest
    def queries(first):
        mixing.extend(call(
            query_kernel,
            (
                shape((heads, length, DV), F32),
                shape((heads, length, DK), BF16),
                shape((heads, length, DV), F32),
            ),
            (
                *(scalars, inputs[3], inputs[2], inputs[1], q_gdn, inputs[0], z_gdn, gain_in),
                *(after(fresh, first), erased),
            ),
            work,
        ))
        return mixing[:1]

    mixing = []
    queries(fresh)
    for hop in range(2, devices - 1):
        got = [after(arrived[-1][0], mixing[0]), *arrived[-1][1:]] if hop == 2 else arrived[-1]
        leaving = combined(got, carry, added)
        arrived.append(hand_on(hop, leaving))
    local_out, reach, gain = mixing

    layout, sections = [], []
    for distance, got in enumerate(units, 1):
        for turn in range(sharers):
            layout.append((distance, turn))
            sections.append(swapped(after(got, leaving[-1]), turn) if turn else got)
    attn_out = call(
        functools.partial(attention_kernel, (devices // 2 + 1) * length, layout),
        shape(q_attn.shape, BF16),
        (scalars, inputs[3], q_attn, gate_attn, k_attn, v_attn, *sections),
        4 * local_heads * length * length * (wanted + 1) * HD_A,
    )
    ready = []
    for at in range(pieces):
        states = [got[at] for got in arrived]
        operands = (*states, after(local_out, attn_out), reach, gain)
        cost = 2 * piece * length * DK * DV
        if at < pieces - 1:
            ready.append(
                call(
                    functools.partial(piece_kernel, at * piece, len(states)),
                    shape((length, piece * DV), BF16),
                    operands,
                    cost,
                    0,
                )
            )
    return call(
        functools.partial(output_kernel, at * piece, len(states)),
        (shape(v_gdn.shape, BF16), shape(q_attn.shape, BF16)),
        (*operands, attn_out, *ready),
        cost,
        0,
        scratch=[pltpu.VMEM((length, piece * DV), BF16), pltpu.SemaphoreType.DMA((pieces + 1,))],
        held=pltpu.HBM,
    )


def solution(mesh):
    tokens = P(("groups", "seq"))
    both = P(("groups", "seq"), "head")
    return jax.shard_map(
        shards,
        mesh=mesh,
        in_specs=(
            tokens,
            both,
            both,
            both,
            both,
            P("head", ("groups", "seq")),
            P("head", ("groups", "seq")),
            P(),
            both,
            P(("groups", "seq"), None),
            P(("groups", "seq"), None),
            both,
        ),
        out_specs=(both, both),
        check_vma=False,
    )
```

```python
import functools

import jax
import jax.numpy as jnp
from jax import lax
from jax.experimental import pallas as pl
from jax.experimental.pallas import tpu as pltpu
from jax.sharding import PartitionSpec as P

DK = 128
DV = 128
QH = 16
KVH = 2
HD_A = 256
EPS = 1e-06
VMEM_LIMIT = 48 * 1024 * 1024
PIECES = 2

F32 = jnp.float32
BF16 = jnp.bfloat16


def dot(a, b):
    return jnp.dot(a, b, preferred_element_type=F32)


def dot_t(a, b):
    return lax.dot_general(a, b, (((1,), (1,)), ((), ())), preferred_element_type=F32)


def prefix_sums(rows):
    count, length = rows.shape
    first = rows.astype(BF16)
    rest = rows - first.astype(F32)
    second = rest.astype(BF16)
    third = (rest - second.astype(F32)).astype(BF16)
    t_at = lax.broadcasted_iota(jnp.int32, (length, length), 0)
    i_at = lax.broadcasted_iota(jnp.int32, (length, length), 1)
    ones = (t_at <= i_at).astype(F32).astype(BF16)
    return dot(first, ones) + dot(second, ones) + dot(third, ones)


def columns_of(rows):
    count, length = rows.shape
    padded = jnp.concatenate([rows, jnp.zeros((length - count, length), F32)], axis=0)
    return padded.T


def diagonal_row(square, same_place):
    return jnp.sum(jnp.where(same_place, square, 0.0), axis=0, keepdims=True)


def places(length):
    row = lax.broadcasted_iota(jnp.int32, (length, length), 0)
    col = lax.broadcasted_iota(jnp.int32, (length, length), 1)
    return row, col


def upper_rows(square, size):
    return jnp.concatenate([square[i : i + size] for i in range(size, square.shape[0], 2 * size)], axis=0)


def state_terms(scalar_ref, inputs, u_ref, w_ref=None, a_ref=None, m_ref=None, send_refs=(), late=()):
    k_ref, gate_ref, beta_ref, doc_ref, v_ref = inputs
    doc = doc_ref[...]
    anchor = scalar_ref[0]
    length = k_ref.shape[0]
    heads = beta_ref.shape[0]
    key_heads = k_ref.shape[1] // DK
    repeat = heads // key_heads
    row, col = places(length)
    beta = jax.nn.sigmoid(beta_ref[...])
    running = prefix_sums(gate_ref[...])
    keys = [k_ref[:, g * DK : (g + 1) * DK] for g in range(key_heads)]
    grams = [dot_t(k, k) for k in keys]
    squares = [diagonal_row(g, row == col) + EPS for g in grams]
    log_inv = [-0.5 * jnp.log(s) for s in squares]
    inv = [lax.rsqrt(s) for s in squares]
    log_rows = jnp.concatenate([log_inv[h // repeat] for h in range(heads)], axis=0)
    cols = columns_of(
        jnp.concatenate([running + log_rows, jnp.broadcast_to(doc.astype(F32), (8, length))], axis=0)
    )
    doc_col = cols[:, heads : heads + 1]
    place = (anchor + col).astype(F32)
    strict = (doc_col <= place) & (col < row)
    tail_same = doc[:, length - 1 : length] <= (anchor + col[:1, :])
    systems = []
    for h in range(heads):
        spread = cols[:, h : h + 1] - running[h : h + 1, :]
        decay = jnp.where(strict, jnp.exp(spread), 0.0)
        weight = beta[h : h + 1, :] * inv[h // repeat]
        systems.append(decay * grams[h // repeat] * weight)
    differ = row ^ col
    diagonal = differ < 8
    strip_row = lax.broadcasted_iota(jnp.int32, (8, length), 0)
    strip_col = lax.broadcasted_iota(jnp.int32, (8, length), 1)
    lead = strip_col // 8 * 8
    unit = jnp.where(strip_row == strip_col - lead, 1.0, 0.0)
    strips = []
    for n in systems:
        kept = jnp.where(diagonal, n, 0.0)
        parts = [kept[at : at + 8] for at in range(0, length, 8)]
        while len(parts) > 1:
            parts = [x + y for x, y in zip(parts[::2], parts[1::2])]
        strips.append(parts[0])
    solved = [unit] * heads
    for step in range(7):
        picked = [jnp.take_along_axis(n, lead + step, axis=1) for n in strips]
        solved = [x - p * x[step : step + 1] for x, p in zip(solved, picked)]
    inverse = [jnp.where(diagonal, jnp.concatenate([x] * (length // 8), axis=0), 0.0) for x in solved]
    level = 3
    while (1 << level) < length:
        size = 1 << level
        starts = range(size, length, 2 * size)
        mask = (upper_rows(differ, size) >> level) == 1
        kept = [jnp.where(mask, upper_rows(n, size), 0.0).astype(BF16) for n in systems]
        inner = [dot(n, x.astype(BF16)) for n, x in zip(kept, inverse)]
        spare = jnp.zeros((size, length), F32)
        inner = [
            jnp.concatenate([p for i in range(len(starts)) for p in (spare, y[i * size : (i + 1) * size])], axis=0)
            for y in inner
        ]
        outer = [dot(upper_rows(x, size).astype(BF16), y.astype(BF16)) for x, y in zip(inverse, inner)]
        inverse = [
            jnp.concatenate(
                [
                    p
                    for j, i in enumerate(starts)
                    for p in (x[i - size : i], x[i : i + size] - o[j * size : (j + 1) * size])
                ],
                axis=0,
            )
            for x, o in zip(inverse, outer)
        ]
        level += 1
    keys_t = [k.astype(F32).T for k in keys]
    for copy in late:
        copy.wait()
    for h in range(heads):
        g = h // repeat
        run = running[h : h + 1, :]
        u = dot(inverse[h].astype(BF16), v_ref[:, h * DV : (h + 1) * DV]).astype(BF16)
        u_ref[h] = u
        tail = jnp.exp(run[:, length - 1 : length] - run)
        tail = jnp.where(tail_same, tail, 0.0) * beta[h : h + 1, :] * inv[g]
        tail_keys = (keys_t[g] * tail).astype(BF16)
        a = dot(tail_keys, u)
        if send_refs:
            piece = heads // len(send_refs)
            send_refs[h // piece][h % piece] = a.astype(BF16)
            continue
        a_ref[h] = a
        entry = jnp.where(doc < anchor, jnp.exp(run), 0.0)
        w = dot((inverse[h] * (entry * inv[g])).astype(BF16), keys[g]).astype(BF16)
        w_ref[h] = w
        m_ref[h] = (jnp.where(row == col, entry[:, length - 1 : length], 0.0) - dot(tail_keys, w)).astype(BF16)


def opening_kernel(scalar_ref, *refs):
    sources, u_ref, send_refs = refs[:5], refs[5], refs[6:-6]
    inputs, sems = refs[-6:-1], refs[-1]

    @pl.when(scalar_ref[0] == 0)
    def _():
        copies = [pltpu.make_async_copy(a, b, sems.at[i]) for i, (a, b) in enumerate(zip(sources, inputs))]
        for copy in copies:
            copy.start()
        for copy in copies[:-1]:
            copy.wait()
        state_terms(scalar_ref, inputs, u_ref, send_refs=send_refs, late=copies[-1:])


def second_kernel(scalar_ref, *refs):
    inputs, (ka_ref, va_ref, gain_ref, _) = refs[:5], refs[5:9]
    u_ref, w_ref, a_ref, m_ref, unit_ref, kept_ref = refs[9:]
    kept_ref[...] = gain_ref[...]
    length = u_ref.shape[1]
    groups = HD_A // DK
    rows = unit_ref.shape[0] // (2 * groups)
    begin = pl.multiple_of(scalar_ref[2], rows)
    for at in range(2 * groups):
        lanes = pl.ds(pl.multiple_of(scalar_ref[1] + at % groups * DK, DK), DK)
        unit_ref[at * rows : (at + 1) * rows] = (ka_ref, va_ref)[at // groups][pl.ds(begin, rows), lanes]

    @pl.when(scalar_ref[0] == 0)
    def _():
        w_ref[...] = jnp.zeros(w_ref.shape, BF16)

    @pl.when(scalar_ref[0] == length)
    def _():
        state_terms(scalar_ref, inputs, u_ref, w_ref, a_ref, m_ref)


def later_kernel(scalar_ref, *refs):
    inputs, outs = refs[:5], refs[9:]
    length = outs[0].shape[1]

    @pl.when(scalar_ref[0] > length)
    def _():
        state_terms(scalar_ref, inputs, *outs)


def query_kernel(
    scalar_ref, doc_ref, beta_ref, gate_ref, q_ref, k_ref, z_ref, gain_ref, u_ref, w_ref, local_ref, reach_ref, gz_ref
):
    length = k_ref.shape[0]
    heads = beta_ref.shape[0]
    key_heads = k_ref.shape[1] // DK
    repeat = heads // key_heads
    anchor = scalar_ref[0]
    row, col = places(length)
    beta = jax.nn.sigmoid(beta_ref[...])
    running = prefix_sums(gate_ref[...])
    doc = doc_ref[...]
    keys = [k_ref[:, g * DK : (g + 1) * DK] for g in range(key_heads)]
    queries = [q_ref[:, g * DK : (g + 1) * DK] for g in range(key_heads)]
    inv = [lax.rsqrt(diagonal_row(dot_t(k, k), row == col) + EPS) for k in keys]
    log_q = [-0.5 * jnp.log(diagonal_row(dot_t(q, q), row == col) + EPS) for q in queries]
    log_rows = jnp.concatenate([log_q[h // repeat] for h in range(heads)], axis=0)
    cols = columns_of(
        jnp.concatenate([running + log_rows, jnp.broadcast_to(doc.astype(F32), (8, length))], axis=0)
    )
    doc_col = cols[:, heads : heads + 1]
    place = (anchor + col).astype(F32)
    same = (doc_col <= place) & (col <= row)
    alive_col = doc_col < anchor.astype(F32)
    cross = [dot_t(q, k) for q, k in zip(queries, keys)]
    for h in range(heads):
        g = h // repeat
        weight = beta[h : h + 1, :] * inv[g]
        decay = jnp.where(same, jnp.exp(cols[:, h : h + 1] - running[h : h + 1, :]), 0.0)
        scores = (decay * cross[g] * weight).astype(BF16)
        local_ref[h] = dot(scores, u_ref[h])
        lead = jnp.where(alive_col, jnp.exp(cols[:, h : h + 1]), 0.0)
        reach_ref[h] = (lead * queries[g].astype(F32) - dot(scores, w_ref[h])).astype(BF16)
    z = z_ref[...].astype(F32)
    gate = z / (1.0 + jnp.exp(-z))
    for h in range(heads):
        gz_ref[h] = gate[:, h * DV : (h + 1) * DV] * gain_ref[...]


def combine_kernel(begin, s_ref, m_ref, a_ref, out_ref):
    for h in range(s_ref.shape[0]):
        out_ref[h] = (dot(m_ref[begin + h], s_ref[h]) + a_ref[begin + h]).astype(BF16)


def normed_piece(begin, states, local_ref, reach_ref, gz_ref, out_ref, columns):
    for at in range(states[0].shape[0]):
        state = states[0][at]
        for other in states[1:]:
            state = state + other[at]
        h = begin + at
        mixed = local_ref[h] + dot(reach_ref[h], state)
        factor = lax.rsqrt(jnp.mean(mixed * mixed, axis=-1, keepdims=True) + EPS)
        spot = columns + at * DV
        out_ref[:, spot : spot + DV] = (mixed * factor * gz_ref[h]).astype(BF16)


def piece_kernel(begin, hops, *refs):
    normed_piece(begin, refs[:hops], *refs[hops:], 0)


def output_kernel(begin, hops, *refs):
    states, terms, attn_ref, ready = refs[:hops], refs[hops : hops + 3], refs[hops + 3], refs[hops + 4 : -4]
    out_hbm, attn_hbm, held_ref, sems = refs[-4:]
    copies = [pltpu.make_async_copy(attn_ref, attn_hbm, sems.at[len(ready) + 1])]
    copies[0].start()
    spot = 0
    for at, part in enumerate((*ready, held_ref)):
        if part is held_ref:
            normed_piece(begin, states, *terms, held_ref, 0)
        width = part.shape[1]
        copies.append(pltpu.make_async_copy(part, out_hbm.at[:, spot : spot + width], sems.at[at]))
        copies[-1].start()
        spot += width
    for copy in copies:
        copy.wait()


def attention_kernel(window, layout, scalar_ref, doc_ref, q_ref, gate_ref, k_ref, v_ref, *refs):
    units, out_ref = refs[:-1], refs[-1]
    length = q_ref.shape[0]
    heads = q_ref.shape[1] // HD_A
    groups = HD_A // DK
    anchor = scalar_ref[0]
    docs = columns_of(jnp.broadcast_to(doc_ref[...].astype(F32), (8, length)))[:, :1].astype(jnp.int32)
    q_place = anchor + lax.broadcasted_iota(jnp.int32, (length, 1), 0)
    lower = jnp.maximum(jnp.maximum(docs, q_place - window + 1), 0)
    spots = [anchor + lax.broadcasted_iota(jnp.int32, (length, length), 1)]
    wanted = pl.ds(pl.multiple_of(scalar_ref[1], HD_A), HD_A)
    keys, values = [k_ref[:, wanted]], [v_ref[:, wanted]]
    for (distance, turn), unit in zip(layout, units):
        rows = unit.shape[0] // (2 * groups)
        start = anchor - distance * length + scalar_ref[2 + turn]
        spots.append(start + lax.broadcasted_iota(jnp.int32, (length, rows), 1))
        blocks = [unit[at * rows : (at + 1) * rows] for at in range(2 * groups)]
        keys.append(jnp.concatenate(blocks[:groups], axis=1))
        values.append(jnp.concatenate(blocks[groups:], axis=1))
    k_place = jnp.concatenate(spots, axis=1)
    visible = (k_place >= lower) & (k_place <= q_place)
    keys = jnp.concatenate(keys, axis=0)
    values = jnp.concatenate(values, axis=0)
    step = 2
    for first in range(0, heads, step):
        names = range(first, min(first + step, heads))
        queries = jnp.concatenate([q_ref[:, h * HD_A : (h + 1) * HD_A] for h in names], axis=0)
        scores = dot_t(queries * BF16(HD_A**-0.5), keys)
        scores = jnp.where(jnp.concatenate([visible] * len(names), axis=0), scores, -jnp.inf)
        peak = jnp.max(scores, axis=-1, keepdims=True)
        weights = jnp.exp(scores - peak)
        total = jnp.sum(weights, axis=-1, keepdims=True)
        mixed = dot(weights.astype(BF16), values)
        for at, h in enumerate(names):
            part = slice(h * HD_A, (h + 1) * HD_A)
            rows = slice(at * length, (at + 1) * length)
            gate = 1.0 + jnp.exp(-gate_ref[:, part].astype(F32))
            out_ref[:, part] = (mixed[rows] / (total[rows] * gate)).astype(BF16)


def call(kernel, out_shape, operands, flops, scalars=1, outside=0, scratch=(), aliases=None, held=pltpu.VMEM):
    moved = sum(o.size * o.dtype.itemsize for o in operands)
    inside = len(operands) - scalars - outside
    operands = [
        pltpu.with_memory_space_constraint(o, pltpu.HBM) if scalars <= i < scalars + outside else o
        for i, o in enumerate(operands)
    ]
    specs = [pl.BlockSpec(memory_space=pltpu.SMEM)] * scalars
    specs += [pl.BlockSpec(memory_space=pltpu.HBM)] * outside
    specs += [pl.BlockSpec(memory_space=pltpu.VMEM)] * inside
    if held is not pltpu.VMEM and aliases:
        specs[-1] = pl.BlockSpec(memory_space=held)
    return pl.pallas_call(
        kernel,
        out_shape=out_shape,
        in_specs=specs,
        out_specs=jax.tree.map(lambda _: pl.BlockSpec(memory_space=held), out_shape),
        scratch_shapes=scratch,
        input_output_aliases=aliases or {},
        compiler_params=pltpu.CompilerParams(vmem_limit_bytes=VMEM_LIMIT),
        cost_estimate=pl.CostEstimate(flops=flops, bytes_accessed=moved, transcendentals=0),
    )(*operands)


def after(value, *others):
    return lax.optimization_barrier((value, *others))[0]


def shards(
    doc_start,
    q_gdn,
    k_gdn,
    v_gdn,
    z_gdn,
    beta_logit,
    log_decay,
    norm_weight,
    q_attn,
    k_attn,
    v_attn,
    gate_attn,
):
    devices = lax.axis_size("seq")
    length = q_gdn.shape[0]
    heads = v_gdn.shape[1] // DV
    local_heads = q_attn.shape[1] // HD_A
    group = QH // KVH
    head_devices = lax.axis_size("head")
    sharers = max(1, min(group // local_heads, head_devices))
    rows = length // sharers
    place = lax.axis_index("seq").astype(jnp.int32)
    head_at = lax.axis_index("head").astype(jnp.int32)
    kv_head = head_at * local_heads // group
    share = head_at % sharers
    scalars = jnp.stack(
        [place * length, kv_head * HD_A] + [(share + sharers - t) % sharers * rows for t in range(sharers)]
    )
    docs = doc_start.reshape(1, length)
    shape = jax.ShapeDtypeStruct
    pieces = PIECES if heads % PIECES == 0 else 1

    sources = (k_gdn, log_decay, beta_logit, docs, v_gdn, norm_weight.reshape(1, DV))
    terms = (
        shape((heads, length, DV), BF16),
        shape((heads, length, DK), BF16),
        shape((heads, DK, DV), F32),
        shape((heads, DK, DK), BF16),
    )
    work = 100 * heads * length * DK * DV
    piece = heads // pieces
    groups = HD_A // DK
    inputs, gain_in = sources[:5], sources[5]
    fresh, *leaving = call(
        opening_kernel,
        (terms[0], *[shape((piece, DK, DV), BF16)] * pieces),
        (scalars, *inputs),
        work,
        outside=len(inputs),
        scratch=[*[pltpu.VMEM(a.shape, a.dtype) for a in inputs], pltpu.SemaphoreType.DMA((len(inputs),))],
    )

    def hand_on(hop, pieces_out):
        return [lax.ppermute(s, "seq", [(hop, hop + 1)]) for s in pieces_out]

    def combined(got, carry, added, between=None):
        done = []
        for at, state in enumerate(got):
            if at == 1 and between:
                state = after(state, *between(done[0]))
            elif done:
                state = after(state, done[-1])
            done.append(
                call(
                    functools.partial(combine_kernel, at * piece),
                    shape((piece, DK, DV), BF16),
                    (state, carry, added),
                    2 * piece * DK * DK * DV,
                    0,
                )
            )
        return done

    def swapped(got, turn):
        pairs = [(i, i // sharers * sharers + (i + turn) % sharers) for i in range(head_devices)]
        return lax.ppermute(got, "head", pairs)

    wanted = min(devices // 2 + 1, devices - 1)
    arrived = [hand_on(0, leaving)]
    fresh, erased, added, carry, unit, gain_in = call(
        second_kernel,
        (*terms, shape((2 * groups * rows, DK), BF16), shape(gain_in.shape, F32)),
        (scalars, *inputs, k_attn, v_attn, gain_in, fresh),
        work,
        aliases={9: 0},
    )
    units = [lax.ppermute(unit, "seq", [(i, i + 1) for i in range(devices - 1)])]
    direct = wanted == devices - 1 and wanted > 1
    leaving = combined(arrived[-1], carry, added)
    arrived.append(hand_on(1, leaving))
    farthest = [lax.ppermute(after(unit, leaving[-1]), "seq", [(0, wanted)])] if direct else []
    fresh, erased, added, carry = call(
        later_kernel,
        terms,
        (scalars, *inputs, after(fresh, leaving[-1]), erased, added, carry),
        work,
        aliases={6: 0, 7: 1, 8: 2, 9: 3},
    )
    block = after(units[0], fresh)
    for distance in range(2, wanted + 1 - direct):
        block = lax.ppermute(block, "seq", [(i, i + 1) for i in range(distance - 1, devices - 1)])
        units.append(block)
    units += farthest
    def queries(first):
        mixing.extend(call(
            query_kernel,
            (
                shape((heads, length, DV), F32),
                shape((heads, length, DK), BF16),
                shape((heads, length, DV), F32),
            ),
            (
                *(scalars, inputs[3], inputs[2], inputs[1], q_gdn, inputs[0], z_gdn, gain_in),
                *(after(fresh, first), erased),
            ),
            work,
        ))
        return mixing[:1]

    mixing = []
    queries(fresh)
    for hop in range(2, devices - 1):
        got = [after(arrived[-1][0], mixing[0]), *arrived[-1][1:]] if hop == 2 else arrived[-1]
        leaving = combined(got, carry, added)
        arrived.append(hand_on(hop, leaving))
    local_out, reach, gain = mixing

    layout, sections = [], []
    for distance, got in enumerate(units, 1):
        for turn in range(sharers):
            layout.append((distance, turn))
            sections.append(swapped(after(got, leaving[-1]), turn) if turn else got)
    attn_out = call(
        functools.partial(attention_kernel, (devices // 2 + 1) * length, layout),
        shape(q_attn.shape, BF16),
        (scalars, inputs[3], q_attn, gate_attn, k_attn, v_attn, *sections),
        4 * local_heads * length * length * (wanted + 1) * HD_A,
    )
    ready = []
    for at in range(pieces):
        states = [got[at] for got in arrived]
        operands = (*states, after(local_out, attn_out), reach, gain)
        cost = 2 * piece * length * DK * DV
        if at < pieces - 1:
            ready.append(
                call(
                    functools.partial(piece_kernel, at * piece, len(states)),
                    shape((length, piece * DV), BF16),
                    operands,
                    cost,
                    0,
                )
            )
    return call(
        functools.partial(output_kernel, at * piece, len(states)),
        (shape(v_gdn.shape, BF16), shape(q_attn.shape, BF16)),
        (*operands, attn_out, *ready),
        cost,
        0,
        scratch=[pltpu.VMEM((length, piece * DV), BF16), pltpu.SemaphoreType.DMA((pieces + 1,))],
        held=pltpu.HBM,
    )


def solution(mesh):
    tokens = P(("groups", "seq"))
    both = P(("groups", "seq"), "head")
    return jax.shard_map(
        shards,
        mesh=mesh,
        in_specs=(
            tokens,
            both,
            both,
            both,
            both,
            P("head", ("groups", "seq")),
            P("head", ("groups", "seq")),
            P(),
            both,
            P(("groups", "seq"), None),
            P(("groups", "seq"), None),
            both,
        ),
        out_specs=(both, both),
        check_vma=False,
    )
```
